32 devices in a mesh: chain: 4 (over y, core), sector: 8 (over z, x).
Axes of the slice: x: 2, y: 2, z: 4, core: 2. Of those that a mesh axis runs over, the one named last changes fastest.
Arguments:
- site_tensors: bfloat16 [8, 8, 128, 4, 128], P('chain', 'sector'), may hold values from -0.5 to 0.5
- mpo: bfloat16 [8, 42, 42, 4, 4], P('chain'), may hold values from -0.75 to 0.75
- left_in: bfloat16 [4, 8, 42, 128, 128], P('chain', 'sector'), may hold values from -6 to 6
- right_in: bfloat16 [4, 8, 42, 128, 128], P('chain', 'sector'), may hold values from -6 to 6
- tile_rows: int32 [9, 8], replicated, may hold values from 32 to 128
Outputs:
- left_envs: bfloat16 [8, 8, 42, 128, 128], P('chain', 'sector')
- right_envs: bfloat16 [8, 8, 42, 128, 128], P('chain', 'sector')
- left_edge: bfloat16 [4, 8, 42, 128, 128], P('chain', 'sector')
The draws below stay inside these ranges and needn't reach their ends.
All inputs are finite; a program needn't handle non-finite values.
Results may differ from the reference program's by a relative error of at most 0.009.
Values may be sent and summed in bfloat16 or wider, within the bound.
No kernel may reach another device: no remote copies, remote signals or barrier semaphores. Data moves between devices by JAX's collectives and lax.ppermute only.
A program may use at most 128 MiB of HBM per device.

```python
import jax
import jax.numpy as jnp
from jax import lax

W = 42
TILE = 128
PHYS = 4
SD = 2
TILES = 8
SITES = 8
BONDS = 9
N_CHAIN = 4


def plant(entries, key, smallest, largest):
    longest = entries.shape.index(max(entries.shape))
    spots = []
    for shift in (0, 1):
        where = [jax.random.randint(jax.random.fold_in(key, axis), (), 0, length) for axis, length in enumerate(entries.shape)]
        where[longest] = (where[longest] + shift) % entries.shape[longest]
        spots.append(tuple(where))
    return entries.at[spots[0]].set(smallest).at[spots[1]].set(largest)


def block_scale(stream_key, extent, split, smallest, high):
    factor_of = 1.0
    for axis_at, blocks in split:
        steps = jax.random.uniform(jax.random.fold_in(jax.random.fold_in(stream_key, 6), axis_at), (blocks,), jnp.float32, smallest / len(split), high / len(split))
        factor_of = factor_of * jnp.repeat(jnp.exp(steps), extent[axis_at] // blocks).reshape((-1,) + (1,) * (len(extent) - 1 - axis_at))
    return factor_of


def noise(key, extent, scale, bound, split=(), kind=jnp.bfloat16):
    values = scale * jax.random.normal(key, extent, jnp.float32)
    if split:
        values = values * block_scale(key, extent, split, -0.22, 0.18)
    return jnp.clip(values, -bound, bound).astype(kind)


def setup_inputs(seed: int = 0) -> dict:
    streams_of = jax.random.split(jax.random.key(seed), 6)
    site_tensors = noise(streams_of[0], (SITES, TILES, TILE, PHYS, TILE), TILE ** -0.5, 0.5, ((0, 4), (1, 8)))
    mpo = noise(streams_of[1], (SITES, W, W, PHYS, PHYS), (3 * W // 2) ** -0.5, 0.75, ((0, 4),))
    left_in = noise(streams_of[2], (N_CHAIN, TILES, W, TILE, TILE), 1.0, 6.0, ((0, 4), (1, 8)))
    right_in = noise(streams_of[3], (N_CHAIN, TILES, W, TILE, TILE), 1.0, 6.0, ((0, 4), (1, 8)))
    tile_rows = plant(jax.random.randint(streams_of[4], (BONDS, TILES), TILE // 4, TILE + 1), jax.random.fold_in(streams_of[4], 1), TILE // 4, TILE).astype(jnp.int32)
    return dict(site_tensors=site_tensors, mpo=mpo, left_in=left_in, right_in=right_in, tile_rows=tile_rows)


charge_groups = ((0, 1), (1, 3), (3, 4))


def mask_part(tensor, rows_left, rows_right, lower, upper):
    tile = tensor.shape[0]
    ids = jnp.arange(tile, dtype=jnp.int32)
    keep = (ids[:, None, None] < rows_left) & (ids[None, None, :] < rows_right)
    return jnp.where(keep, tensor[:, lower:upper, :], jnp.zeros((), tensor.dtype))


def left_tile(env, tensor, mpo_site, rows_left, rows_next):
    tile = tensor.shape[0]
    width = env.shape[0]
    full = jnp.concatenate([mask_part(tensor, rows_left, rows_next[n], lo, hi) for n, (lo, hi) in enumerate(charge_groups)], axis=1)
    prod = jnp.dot(env.reshape(width * tile, tile), full.reshape(tile, 4 * tile), preferred_element_type=jnp.float32)
    prod = prod.astype(jnp.bfloat16).reshape(width, tile, 4, tile)
    terms = []
    for lo, hi in charge_groups:
        inner = jnp.einsum("wvst,wxtb->vxsb", mpo_site[:, :, lo:hi, lo:hi].astype(jnp.float32), prod[:, :, lo:hi, :].astype(jnp.float32)).astype(jnp.bfloat16)
        terms.append(jnp.einsum("xsy,vxsb->vyb", full[:, lo:hi, :].astype(jnp.float32), inner.astype(jnp.float32)))
    return terms[0], terms[1], terms[2]


def right_tile(sources, tensor, mpo_site, rows_left, rows_next):
    tile = tensor.shape[0]
    width = sources[0].shape[0]
    total = jnp.zeros((width, tile, tile), jnp.float32)
    for n, (lo, hi) in enumerate(charge_groups):
        part = mask_part(tensor, rows_left, rows_next[n], lo, hi)
        count = hi - lo
        prod = jnp.dot(sources[n].reshape(width * tile, tile), part.reshape(tile * count, tile).T, preferred_element_type=jnp.float32)
        prod = prod.astype(jnp.bfloat16).reshape(width, tile, tile, count)
        inner = jnp.einsum("wust,uyat->wyas", mpo_site[:, :, lo:hi, lo:hi].astype(jnp.float32), prod.astype(jnp.float32)).astype(jnp.bfloat16)
        total = total + jnp.einsum("xsy,wyas->wxa", part.astype(jnp.float32), inner.astype(jnp.float32))
    return total.astype(jnp.bfloat16)


def next_rows(rows_there):
    count = rows_there.shape[0]
    padded = jnp.concatenate([rows_there, jnp.zeros((2,), jnp.int32)])
    return jnp.stack([padded[n:n + count] for n in range(3)], axis=1)


def left_site(env_all, tensors, mpo_site, rows_here, rows_there):
    rows_next = next_rows(rows_there)
    first, second, third = jax.vmap(left_tile, in_axes=(0, 0, None, 0, 0))(env_all, tensors, mpo_site, rows_here, rows_next)
    second = lax.optimization_barrier(second.astype(jnp.bfloat16)).astype(jnp.float32)
    third = lax.optimization_barrier(third.astype(jnp.bfloat16)).astype(jnp.float32)
    moved_one = jnp.concatenate([jnp.zeros_like(second[:1]), second[:-1]], axis=0)
    moved_two = jnp.concatenate([jnp.zeros_like(third[:2]), third[:-2]], axis=0)
    return (first + moved_one + moved_two).astype(jnp.bfloat16)


def right_site(env_all, tensors, mpo_site, rows_here, rows_there):
    rows_next = next_rows(rows_there)
    count = env_all.shape[0]
    padded = jnp.concatenate([env_all, jnp.zeros((2,) + env_all.shape[1:], env_all.dtype)], axis=0)
    sources = (padded[0:count], padded[1:count + 1], padded[2:count + 2])
    return jax.vmap(right_tile, in_axes=(0, 0, None, 0, 0))(sources, tensors, mpo_site, rows_here, rows_next)


def reference(site_tensors, mpo, left_in, right_in, tile_rows):
    lefts = []
    rights = [None] * SITES
    for segment in range(N_CHAIN):
        env = left_in[segment]
        for inner in range(SD):
            site = segment * SD + inner
            env = left_site(env, site_tensors[site], mpo[site], tile_rows[site], tile_rows[site + 1])
            lefts.append(env)
    for segment in range(N_CHAIN):
        env = right_in[segment]
        for inner in reversed(range(SD)):
            site = segment * SD + inner
            env = right_site(env, site_tensors[site], mpo[site], tile_rows[site], tile_rows[site + 1])
            rights[site] = env
    left_envs = jnp.stack(lefts)
    right_envs = jnp.stack(rights)
    left_edge = jnp.concatenate([left_in[:1], left_envs[SD - 1::SD][:N_CHAIN - 1]], axis=0)
    return left_envs, right_envs, left_edge
```

```python
import functools

import jax
import jax.numpy as jnp
from jax import lax
from jax.experimental import pallas as pl
from jax.experimental.pallas import tpu as pltpu
from jax.sharding import PartitionSpec as P

f32 = jnp.float32
bf16 = jnp.bfloat16
AXES = ("chain", "sector")
GROUP = 8
STEP_ROWS = 2 * GROUP
LOAD_ROWS = 32
ANY = pl.BlockSpec(memory_space=pl.ANY)
SMEM = pl.BlockSpec(memory_space=pltpu.SMEM)
VMEM = pl.BlockSpec(memory_space=pltpu.VMEM)
LIMIT = 56 * 2**20


class Routes:
    def __init__(self, chains, sectors):
        def at(pair, core, z, x):
            return (2 * pair + core) * sectors + 2 * z + x

        pairs, zs = range(chains // 2), range(sectors // 2)
        every = [(y, z, e) for y in pairs for z in zs for e in (0, 1)]
        below = [(y, z, e) for y, z, e in every if z + 1 in zs]
        self.left_cross = [(at(y, e, z, 1 - e), at(y, e, z, e)) for y, z, e in every]
        self.right_cross = [(at(y, e, z, 1 - e), at(y, 1 - e, z, e)) for y, z, e in every]
        self.to_right_core = [(at(y, e, z, e), at(y, 1 - e, z, e)) for y, z, e in every]
        self.left_up = [(at(y, e, z, e), at(y, e, z + 1, e)) for y, z, e in below]
        self.right_down = [(at(y, 1 - e, z + 1, e), at(y, 1 - e, z, e)) for y, z, e in below]
        self.right_native_down = [(at(y, e, z + 1, e), at(y, 1 - e, z, e)) for y, z, e in below]
        self.left_back = [(b, a) for a, b in self.left_cross]
        self.right_back = [(b, a) for a, b in self.right_cross]
        self.from_right_core = [(b, a) for a, b in self.to_right_core]
        shifts = [(c, q) for c in range(chains - 1) for q in range(sectors)]
        self.edge_same = [(c * sectors + q, (c + 1) * sectors + q) for c, q in shifts if c % 2 == q % 2]
        self.edge_other = [(c * sectors + q, (c + 1) * sectors + q) for c, q in shifts if c % 2 != q % 2]


def move(block, route):
    return lax.ppermute(block, AXES, route)


def prepare_body(left, width, tile, steps, info, table, here, there, k0, k1, k3, *outs):
    first, z, x = info[0], info[1], info[2]
    count = table.shape[1]
    local, remote = outs[0:4], outs[4:8]
    small_local, large, small_remote = outs[8:11]

    def rows(bond, index):
        safe = jnp.clip(index, 0, count - 1)
        return jnp.where((index >= 0) & (index < count), table[bond, safe], 0)

    sub = lax.broadcasted_iota(jnp.int32, (tile, tile), 0)
    lane = lax.broadcasted_iota(jnp.int32, (tile, tile), 1)
    sign = 1 if left else -1
    u = 2 * z if left else 2 * z + 1
    v = u + sign
    for step in range(steps):
        site = step if left else steps - 1 - step
        source_bond = first + (site if left else site + 1)
        target_bond = first + (site + 1 if left else site)
        u_first = (x == 0) if left else (x == 1)

        def tensor(pair, which, state):
            a = pair[0, site, state]
            b = pair[1, site, state]
            flag = u_first if which == 0 else jnp.logical_not(u_first)
            return jnp.where(flag, a.astype(f32), b.astype(f32))

        def factor(pair, which, state, source, target):
            a = tensor(pair, which, state)
            if not left:
                a = a.T
            keep = (sub < rows(source_bond, source)) & (lane < rows(target_bond, target))
            return jnp.where(keep, a, 0.0)

        def store(refs, dual, mono):
            for i, m in enumerate(dual):
                refs[0][step, :, i * tile : (i + 1) * tile] = m.astype(bf16)
            refs[1][step] = mono.astype(bf16)
            refs[2][step] = dual[0].T.astype(bf16)
            for i, m in enumerate((dual[1], dual[2], mono)):
                refs[3][step, :, i * tile : (i + 1) * tile] = m.T.astype(bf16)

        up, vp = u - 2 * sign, v - 2 * sign
        store(
            local,
            [factor(here, 0, 0, u, u)] + [factor(here, 0 if left else 1, t, u, v) for t in (1, 2)],
            factor(here, 1, 0, v, v),
        )
        far = there if left else here
        store(
            remote,
            [factor(far, 1, 3, vp, v)] + [factor(far, 1 if left else 0, t, vp, u) for t in (1, 2)],
            factor(far, 0, 3, up, u),
        )

        def spread(k):
            n = k.shape[0]
            tall = lax.broadcasted_iota(jnp.int32, (n * GROUP, n), 0) // GROUP
            tall = jnp.where(tall == lax.broadcasted_iota(jnp.int32, (n * GROUP, n), 1), 1.0, 0.0)
            wide = lax.broadcasted_iota(jnp.int32, (n, n * GROUP), 1) // GROUP
            wide = jnp.where(wide == lax.broadcasted_iota(jnp.int32, (n, n * GROUP), 0), 1.0, 0.0)
            mid = jnp.dot(tall.astype(bf16), k, preferred_element_type=f32).astype(bf16)
            full = jnp.dot(mid, wide.astype(bf16), preferred_element_type=f32)
            i = lax.broadcasted_iota(jnp.int32, full.shape, 0) % GROUP
            j = lax.broadcasted_iota(jnp.int32, full.shape, 1) % GROUP
            return jnp.where(i == j, full, 0.0).astype(bf16)

        small_local[step] = spread(k0[site])
        large[step] = spread(k1[site])
        small_remote[step] = spread(k3[site])


def prepare(left, info, table, here, there, k0, k1, k3):
    steps, tile = here.shape[1], here.shape[-1]
    width = k0.shape[-1]
    n = width * GROUP
    shapes = [(steps, tile, 3 * tile), (steps, tile, tile), (steps, tile, tile), (steps, tile, 3 * tile)] * 2
    shapes += [(steps, n, n), (steps, 2 * n, 2 * n), (steps, n, n)]
    outs = pl.pallas_call(
        functools.partial(prepare_body, left, width, tile, steps),
        in_specs=[SMEM, SMEM] + [VMEM] * 5,
        out_specs=[VMEM] * len(shapes),
        out_shape=[jax.ShapeDtypeStruct(s, bf16) for s in shapes],
        compiler_params=pltpu.CompilerParams(vmem_limit_bytes=LIMIT),
    )(info, table, here, there, k0, k1, k3)
    return (*outs[0:4], outs[8], outs[9]), (*outs[4:8], outs[10], outs[9])


def terms_body(width, tile, step, last, flags, near, cross, bd, bm, cp, cq, ks, kd, *rest):
    if last:
        acc, out_near, out_cross, e_d, e_m, vbd, vbm, vcp, vcq, vks, vkd, z, out, vacc = rest[:14]
    else:
        out_hbm, e_d, e_m, vbd, vbm, vcp, vcq, vks, vkd, z, out = rest[:11]
    load_sem, weight_sem, store_sem = rest[-3:]
    active, dual_near = flags[0], flags[1]
    loads = tile // LOAD_ROWS
    per_load = LOAD_ROWS // STEP_ROWS

    @pl.when(active == 1)
    def _():
        def weight(i, src, dst):
            return pltpu.make_async_copy(src.at[step], dst, weight_sem.at[i])

        weights = [
            weight(i, s, d)
            for i, (s, d) in enumerate(((bd, vbd), (bm, vbm), (ks, vks), (kd, vkd), (cp, vcp), (cq, vcq)))
        ]

        def load(k, src, dst, which):
            r = pl.ds(k * LOAD_ROWS, LOAD_ROWS)
            return pltpu.make_async_copy(src.at[:, r, :], dst.at[:, r, :], load_sem.at[which, k])

        def start_loads(k):
            @pl.when(dual_near == 1)
            def _():
                load(k, near, e_d, 0).start()
                load(k, cross, e_m, 1).start()

            @pl.when(dual_near != 1)
            def _():
                load(k, cross, e_d, 0).start()
                load(k, near, e_m, 1).start()

        for w in weights[:2]:
            w.start()
        start_loads(0)
        for w in weights[2:4]:
            w.start()
        for k in range(1, loads):
            start_loads(k)
        for w in weights[4:]:
            w.start()
        if last:
            accs = [pltpu.make_async_copy(acc.at[i], vacc.at[i], weight_sem.at[6 + i]) for i in range(2)]
            for a in accs:
                a.start()
        for w in weights[:4]:
            w.wait()

        def rows(i):
            r = pl.ds(i * STEP_ROWS, STEP_ROWS)
            yd = jnp.dot(e_d[:, r, :].reshape(width * STEP_ROWS, tile), vbd[...], preferred_element_type=f32)
            ym = jnp.dot(e_m[:, r, :].reshape(width * STEP_ROWS, tile), vbm[...], preferred_element_type=f32)
            yd = yd.reshape(width, STEP_ROWS, 3 * tile)
            ym = ym.reshape(width, STEP_ROWS, tile)
            halves = []
            for h in range(2):
                c = slice(h * GROUP, (h + 1) * GROUP)
                one = jnp.concatenate(
                    [yd[:, c, :tile].reshape(width * GROUP, tile), ym[:, c, :].reshape(width * GROUP, tile)], axis=1
                )
                zh = jnp.dot(vks[...], one.astype(bf16), preferred_element_type=f32)
                halves.append(zh.reshape(width, GROUP, 2 * tile))
            both = jnp.concatenate(halves, axis=1).astype(bf16)
            z[0, :, r, :] = both[:, :, :tile]
            z[3, :, r, :] = both[:, :, tile:]
            two = jnp.concatenate(
                [
                    jnp.concatenate(
                        [
                            yd[:, h * GROUP : (h + 1) * GROUP, t * tile : (t + 1) * tile].reshape(width * GROUP, tile)
                            for h in range(2)
                        ],
                        axis=1,
                    )
                    for t in (1, 2)
                ],
                axis=0,
            )
            zz = jnp.dot(vkd[...], two.astype(bf16), preferred_element_type=f32).reshape(2, width, GROUP, 2 * tile)
            zz = jnp.concatenate([zz[..., :tile], zz[..., tile:]], axis=2).astype(bf16)
            z[1, :, r, :] = zz[0]
            z[2, :, r, :] = zz[1]

        for k in range(loads):
            load(k, near, e_d, 0).wait()
            load(k, near, e_m, 1).wait()
            for i in range(per_load):
                rows(k * per_load + i)
        for w in weights[4:]:
            w.wait()
        if last:
            for a in accs:
                a.wait()

        cuts = [0, width // 6 * 2, width // 6 * 4, width]

        def save(k, which):
            c = pl.ds(cuts[k], cuts[k + 1] - cuts[k])
            sem = store_sem.at[which, k]
            if not last:
                pltpu.make_async_copy(out.at[which, c], out_hbm.at[which, c], sem).start()
                return

            @pl.when((dual_near == 1) == (which == 0))
            def _():
                pltpu.make_async_copy(out.at[which, c], out_near.at[c], sem).start()

            @pl.when((dual_near == 1) != (which == 0))
            def _():
                pltpu.make_async_copy(out.at[which, c], out_cross.at[c], sem).start()

        def saved(k, which):
            c = pl.ds(cuts[k], cuts[k + 1] - cuts[k])
            dst = out_near.at[c] if last else out_hbm.at[which, c]
            pltpu.make_async_copy(out.at[which, c], dst, store_sem.at[which, k]).wait()

        for k in range(3):
            for i in range(cuts[k], cuts[k + 1], 2):
                span = range(i, min(i + 2, cuts[k + 1]))
                p = jnp.dot(vcp[...], jnp.concatenate([z[0, j] for j in span], axis=1), preferred_element_type=f32)
                q = jnp.dot(
                    vcq[...],
                    jnp.concatenate([z[1:4, j].reshape(3 * tile, tile) for j in span], axis=1),
                    preferred_element_type=f32,
                )
                for n, j in enumerate(span):
                    pj, qj = p[:, n * tile : (n + 1) * tile], q[:, n * tile : (n + 1) * tile]
                    if last:
                        pj, qj = pj + vacc[1, j], qj + vacc[0, j]
                    out[0, j] = pj.astype(out.dtype)
                    out[1, j] = qj.astype(out.dtype)
            save(k, 0)
            save(k, 1)
        for k in range(3):
            saved(k, 0)
            saved(k, 1)


def terms(flags, step, near, cross, factors, acc=None):
    width, tile, _ = near.shape
    last = acc is not None
    n = width * GROUP
    out_type = bf16 if last else f32
    env = jax.ShapeDtypeStruct((width, tile, tile), bf16)
    total = jax.ShapeDtypeStruct((2, width, tile, tile), f32)
    scratch = [
        pltpu.VMEM((width, tile, tile), bf16),
        pltpu.VMEM((width, tile, tile), bf16),
        pltpu.VMEM((tile, 3 * tile), bf16),
        pltpu.VMEM((tile, tile), bf16),
        pltpu.VMEM((tile, tile), bf16),
        pltpu.VMEM((tile, 3 * tile), bf16),
        pltpu.VMEM((n, n), bf16),
        pltpu.VMEM((2 * n, 2 * n), bf16),
        pltpu.VMEM((4, width, tile, tile), bf16),
        pltpu.VMEM((2, width, tile, tile), out_type),
    ]
    if last:
        scratch.append(pltpu.VMEM((2, width, tile, tile), f32))
    scratch += [
        pltpu.SemaphoreType.DMA((2, tile // LOAD_ROWS)),
        pltpu.SemaphoreType.DMA((8,)),
        pltpu.SemaphoreType.DMA((2, 3)),
    ]
    operands = [near, cross, *factors] + ([acc] if last else [])
    return pl.pallas_call(
        functools.partial(terms_body, width, tile, step, last),
        in_specs=[SMEM] + [ANY] * len(operands),
        out_specs=[ANY, ANY] if last else ANY,
        out_shape=[env, env] if last else total,
        scratch_shapes=scratch,
        compiler_params=pltpu.CompilerParams(vmem_limit_bytes=LIMIT),
    )(flags, *operands)


def compact(mpo, left):
    order = (0, 3, 2, 4, 1) if left else (0, 3, 1, 4, 2)
    m = jnp.transpose(mpo, order)
    sites, _, width, _, _ = m.shape
    return m[:, 0, :, 0, :], m[:, 1:3, :, 1:3, :].reshape(sites, 2 * width, 2 * width), m[:, 3, :, 3, :]


def shards(site_tensors, mpo, left_in, right_in, tile_rows):
    chains, sectors = lax.axis_size("chain"), lax.axis_size("sector")
    routes = Routes(chains, sectors)
    chain, sector = lax.axis_index("chain"), lax.axis_index("sector")
    core, x = chain % 2, sector % 2
    sites = site_tensors.shape[0]
    same = core == x
    info = jnp.stack([(chain - core + x) * sites, sector // 2, x]).astype(jnp.int32)

    left_near, right_own = left_in[0, 0], right_in[0, 0]
    left_cross = move(left_near, routes.left_cross)
    left_near_below = move(left_near, routes.left_up)
    right_near_above = move(right_own, routes.right_native_down)
    right_near = move(right_own, routes.to_right_core)
    right_cross = move(right_own, routes.right_cross)

    tensors = jnp.transpose(site_tensors[:, 0], (0, 2, 1, 3))
    pair = jnp.stack([tensors, move(tensors, routes.left_cross)])
    pair_below = move(pair, routes.left_up)
    pair_right = move(pair, routes.to_right_core)
    k_left = compact(mpo, True)
    k_right = [move(k, routes.to_right_core) for k in compact(mpo, False)]

    left_cross_below = move(left_cross, routes.left_up)
    right_cross_above = move(right_cross, routes.right_down)

    left_local, left_remote = prepare(True, info, tile_rows, pair, pair_below, *k_left)
    right_local, right_remote = prepare(False, info, tile_rows, pair_right, pair_right, *k_right)

    left_u_near = x == 0
    right_u_near = x == 1

    def flags(on, near):
        return jnp.stack([on, near]).astype(jnp.int32)

    lf_local, lf_remote = flags(same, left_u_near), flags(same, ~left_u_near)
    rf_local, rf_remote = flags(~same, right_u_near), flags(~same, ~right_u_near)

    lefts, rights = [], []
    l_far, r_far = (left_near_below, left_cross_below), (right_near_above, right_cross_above)
    l, r = (left_near, left_cross), (right_near, right_cross)
    for step in range(sites):
        part = terms(lf_local, step, *l, left_local)
        l = terms(lf_remote, step, *l_far, left_remote, part)
        if step + 1 < sites:
            l_far = [move(b, routes.left_up) for b in l]
        back = move(l[1], routes.left_back)
        lefts.append(jnp.where(same, l[0], back))
        if step + 1 == sites:
            edge_near, edge_cross = move(l[0], routes.edge_same), move(back, routes.edge_other)

        part = terms(rf_local, step, *r, right_local)
        r = terms(rf_remote, step, *r_far, right_remote, part)
        if step + 1 < sites:
            r_far = [move(b, routes.right_down) for b in r]
        back = move(r[1], routes.right_back)
        rights.append(jnp.where(same, move(r[0], routes.from_right_core), back))

    left_envs = jnp.stack(lefts)[:, None]
    right_envs = jnp.stack(rights[::-1])[:, None]
    edge = jnp.where(same, edge_cross, edge_near)
    left_edge = jnp.where(chain == 0, left_in[0, 0], edge)[None, None]
    return left_envs, right_envs, left_edge


def solution(mesh):
    placed = (
        P("chain", "sector", None, None, None),
        P("chain", None, None, None, None),
        P("chain", "sector", None, None, None),
        P("chain", "sector", None, None, None),
        P(),
    )
    return jax.shard_map(
        shards,
        mesh=mesh,
        in_specs=placed,
        out_specs=(
            P("chain", "sector", None, None, None),
            P("chain", "sector", None, None, None),
            P("chain", "sector", None, None, None),
        ),
        check_vma=False,
    )
```

```python
import functools

import jax
import jax.numpy as jnp
from jax import lax
from jax.experimental import pallas as pl
from jax.experimental.pallas import tpu as pltpu
from jax.sharding import PartitionSpec as P

f32 = jnp.float32
bf16 = jnp.bfloat16
AXES = ("chain", "sector")
GROUP = 8
STEP_ROWS = 2 * GROUP
ANY = pl.BlockSpec(memory_space=pl.ANY)
SMEM = pl.BlockSpec(memory_space=pltpu.SMEM)
VMEM = pl.BlockSpec(memory_space=pltpu.VMEM)
LIMIT = 18 * 2**20


class Routes:
    def __init__(self, chains, sectors):
        def at(pair, core, z, x):
            return (2 * pair + core) * sectors + 2 * z + x

        pairs, zs = range(chains // 2), range(sectors // 2)
        every = [(y, z, e) for y in pairs for z in zs for e in (0, 1)]
        below = [(y, z, e) for y, z, e in every if z + 1 in zs]
        self.left_cross = [(at(y, e, z, 1 - e), at(y, e, z, e)) for y, z, e in every]
        self.right_cross = [(at(y, e, z, 1 - e), at(y, 1 - e, z, e)) for y, z, e in every]
        self.to_right_core = [(at(y, e, z, e), at(y, 1 - e, z, e)) for y, z, e in every]
        self.left_up = [(at(y, e, z, e), at(y, e, z + 1, e)) for y, z, e in below]
        self.right_down = [(at(y, 1 - e, z + 1, e), at(y, 1 - e, z, e)) for y, z, e in below]
        self.right_native_down = [(at(y, e, z + 1, e), at(y, 1 - e, z, e)) for y, z, e in below]
        self.left_back = [(b, a) for a, b in self.left_cross]
        self.right_back = [(b, a) for a, b in self.right_cross]
        self.from_right_core = [(b, a) for a, b in self.to_right_core]
        shifts = [(c, q) for c in range(chains - 1) for q in range(sectors)]
        self.edge_same = [(c * sectors + q, (c + 1) * sectors + q) for c, q in shifts if c % 2 == q % 2]
        self.edge_other = [(c * sectors + q, (c + 1) * sectors + q) for c, q in shifts if c % 2 != q % 2]


def move(block, route):
    return lax.ppermute(block, AXES, route)


def in_hbm(x):
    return pltpu.with_memory_space_constraint(x, pltpu.HBM)


def in_vmem(x):
    return pltpu.with_memory_space_constraint(x, pltpu.VMEM)


def spread_body(width, steps, info, own, received, *outs):
    def spread(k, states, flip):
        n = len(states) * width * GROUP
        cols = 4 * width
        row = lax.broadcasted_iota(jnp.int32, (n, cols), 0) // GROUP
        col = lax.broadcasted_iota(jnp.int32, (n, cols), 1)
        pick = jnp.where(row + states[0] * width == col, 1.0, 0.0)
        if not flip:
            mid = jnp.dot(pick.astype(bf16), k, preferred_element_type=f32).astype(bf16)
            out = lax.dot_general(
                mid, pick.astype(bf16), (((1,), (1,)), ((), ())), preferred_element_type=f32
            )
        else:
            out = jnp.zeros((n, n), f32)
            group = lax.broadcasted_iota(jnp.int32, (n, width), 0) // GROUP
            inner = lax.broadcasted_iota(jnp.int32, (n, width), 1)
            tall = [jnp.where(group - i * width == inner, 1.0, 0.0).astype(bf16) for i in range(len(states))]
            for i, a in enumerate(states):
                for j, b in enumerate(states):
                    block = k[a * width : (a + 1) * width, b * width : (b + 1) * width]
                    mid = lax.dot_general(
                        tall[i], block, (((1,), (1,)), ((), ())), preferred_element_type=f32
                    ).astype(bf16)
                    out += lax.dot_general(
                        mid, tall[j], (((1,), (1,)), ((), ())), preferred_element_type=f32
                    )
        i = lax.broadcasted_iota(jnp.int32, out.shape, 0) % GROUP
        j = lax.broadcasted_iota(jnp.int32, out.shape, 1) % GROUP
        return jnp.where(i == j, out, 0.0).astype(bf16)

    def fill(source, flip):
        for step in range(steps):
            k = source[steps - 1 - step if flip else step]
            for i, states in enumerate(((0,), (1, 2), (3,))):
                outs[3 * step + i][...] = spread(k, states, flip)

    @pl.when(info[3] == 1)
    def _():
        fill(own, False)

    @pl.when(info[3] != 1)
    def _():
        fill(received, True)


def spread(info, own, received):
    steps, width = own.shape[0], own.shape[1] // 4
    n = width * GROUP
    shapes = [(n, n), (2 * n, 2 * n), (n, n)] * steps
    return pl.pallas_call(
        functools.partial(spread_body, width, steps),
        in_specs=[SMEM, VMEM, VMEM],
        out_specs=[VMEM] * len(shapes),
        out_shape=[pltpu.HBM(s, bf16) for s in shapes],
        compiler_params=pltpu.CompilerParams(vmem_limit_bytes=LIMIT),
    )(info, own, received)


def terms_body(left, last, final, onto, width, tile, step, steps, info, table, pair, single, a_near, a_cross, small, large, *rest):
    joined = single is None
    if last:
        acc, *rest = rest
        if left:
            rest = rest[1:] if onto else rest
            envs, *rest = rest
            *rest, envs_sem = rest
        out_pair = out_near = None
        if not final:
            out_pair, *rest = rest
        if final or not left:
            out_near, *rest = rest
        out_cross, info_out, *rest = rest
    else:
        acc, info_out, *rest = rest
    bd, bm, cp, cq, y0, y1, z, vacc, an, ac, ks, kd, sem, weight_sem, *rest = rest
    first, zpos, x, same = info[0], info[1], info[2], info[3]
    for i in range(info.shape[0]):
        info_out[i] = info[i]
    active = same if left else 1 - same
    u_near = (x == 0) if left else (x == 1)
    cuts = [0, width // 6 * 2, width // 6 * 4, width]
    site = step if left else steps - 1 - step

    def carry(which, k):
        c = pl.ds(cuts[k], cuts[k + 1] - cuts[k])
        ends = (acc.at[which, c], vacc.at[which, c])
        return pltpu.make_async_copy(*(ends if last else ends[::-1]), sem.at[which, k])

    def save(k):
        c = pl.ds(cuts[k], cuts[k + 1] - cuts[k])
        return pltpu.make_async_copy((out_pair if out_near is None else out_near).at[c], envs.at[step, 0, c], envs_sem.at[k])

    carries = [carry(which, k) for k in range(3) for which in range(2)]
    saves = [save(k) for k in range(3)] if last and left else []
    factors = [
        pltpu.make_async_copy(src.at[pl.ds(src.shape[0] - 4 * (steps - site), 4)], dst, weight_sem.at[i])
        for i, (src, dst) in enumerate(((a_near, an), (a_cross, ac)))
    ]
    weights = [
        pltpu.make_async_copy(src, dst, weight_sem.at[2 + i]) for i, (src, dst) in enumerate(((small, ks), (large, kd)))
    ]
    fetches = []
    if rest:
        near, cross, fetch_sem = rest
        for i, dst in enumerate((near, cross)):
            for k in range(3):
                c = pl.ds(cuts[k], cuts[k + 1] - cuts[k])
                if joined:
                    src = pair.at[pl.ds(i * width + cuts[k], cuts[k + 1] - cuts[k])]
                else:
                    src = (pair, single)[i].at[c]
                fetches.append(pltpu.make_async_copy(src, dst.at[c], fetch_sem.at[i, k]))
    elif joined:
        near, cross = pair.at[pl.ds(0, width)], pair.at[pl.ds(width, width)]
    else:
        near, cross = pair, single.at[pl.ds(0, width)]

    @pl.when(active == 1)
    def _():
        for c in factors + fetches + weights + (carries if last else []):
            c.start()
        count = table.shape[1]
        source_bond = first + (site if left else site + 1)
        target_bond = first + (site + 1 if left else site)
        sign = 1 if left else -1
        u = 2 * zpos if left else 2 * zpos + 1
        v = u + sign
        far_u, far_v = u - 2 * sign, v - 2 * sign

        def rows_of(bond, index):
            safe = jnp.clip(index, 0, count - 1)
            return jnp.where((index >= 0) & (index < count), table[bond, safe], 0)

        sub = lax.broadcasted_iota(jnp.int32, (tile, tile), 0)
        lane = lax.broadcasted_iota(jnp.int32, (tile, tile), 1)

        def factor(of_u, state, source, target):
            a = jnp.where(u_near if of_u else jnp.logical_not(u_near), an[state].astype(f32), ac[state].astype(f32))
            a = a if left else a.T
            keep = (sub < rows_of(source_bond, source)) & (lane < rows_of(target_bond, target))
            return jnp.where(keep, a, 0.0)

        for c in factors:
            c.wait()
        if last:
            dual = [factor(False, 3, far_v, v)] + [factor(not left, t, far_v, u) for t in (1, 2)]
            mono = factor(True, 3, far_u, u)
        else:
            dual = [factor(True, 0, u, u)] + [factor(left, t, u, v) for t in (1, 2)]
            mono = factor(False, 0, v, v)
        for i, m in enumerate(dual):
            bd[:, i * tile : (i + 1) * tile] = m.astype(bf16)
        bm[...] = mono.astype(bf16)
        cp[...] = dual[0].T.astype(bf16)
        for i, m in enumerate((dual[1], dual[2], mono)):
            cq[:, i * tile : (i + 1) * tile] = m.T.astype(bf16)

        dual_near = jnp.logical_not(u_near) if last else u_near

        for f in fetches:
            f.wait()
        def products(i, slot):
            r = pl.ds(pl.multiple_of(i * STEP_ROWS, STEP_ROWS), STEP_ROWS)
            e_n, e_c = near[:, r, :], cross[:, r, :]
            e_d = jnp.where(dual_near, e_n, e_c).reshape(width * STEP_ROWS, tile)
            e_m = jnp.where(dual_near, e_c, e_n).reshape(width * STEP_ROWS, tile)
            yd = jnp.dot(e_d, bd[...], preferred_element_type=f32).reshape(width, STEP_ROWS, 3 * tile)
            ym = jnp.dot(e_m, bm[...], preferred_element_type=f32).reshape(width, STEP_ROWS, tile)
            n = width * GROUP
            for h in range(2):
                c = slice(h * GROUP, (h + 1) * GROUP)
                half = slice(h * tile, (h + 1) * tile)
                slot[h * n : (h + 1) * n, :tile] = yd[:, c, :tile].reshape(n, tile).astype(bf16)
                slot[h * n : (h + 1) * n, tile:] = ym[:, c, :].reshape(n, tile).astype(bf16)
                for t in range(2):
                    part = yd[:, c, (1 + t) * tile : (2 + t) * tile].reshape(n, tile)
                    slot[(2 + t) * n : (3 + t) * n, half] = part.astype(bf16)

        def mix(i, slot):
            r = pl.ds(pl.multiple_of(i * STEP_ROWS, STEP_ROWS), STEP_ROWS)
            n = width * GROUP
            halves = [
                jnp.dot(ks[...], slot[h * n : (h + 1) * n, :], preferred_element_type=f32)
                .reshape(width, GROUP, 2 * tile)
                for h in range(2)
            ]
            both = jnp.concatenate(halves, axis=1).astype(bf16)
            z[0, :, r, :] = both[:, :, :tile]
            z[3, :, r, :] = both[:, :, tile:]
            zz = jnp.dot(kd[...], slot[2 * n :, :], preferred_element_type=f32).reshape(2, width, GROUP, 2 * tile)
            zz = jnp.concatenate([zz[..., :tile], zz[..., tile:]], axis=2).astype(bf16)
            z[1, :, r, :] = zz[0]
            z[2, :, r, :] = zz[1]

        count_rows = tile // STEP_ROWS
        products(0, y0)
        for c in weights:
            c.wait()

        def turn(j, _):
            for k in range(2 // 2):
                i = 2 * j + 2 * k
                products(i + 1, y1)
                mix(i, y0)
                products(jnp.minimum(i + 2, count_rows - 2), y0)
                mix(i + 1, y1)
            return 0

        lax.fori_loop(0, count_rows // 2, turn, 0)
        if last:
            for c in carries:
                c.wait()
        for k in range(3):
            def close(m, _, k=k):
                for i in range(7):
                    at = cuts[k] + 2 * (m * 7 + i)
                    p = jnp.dot(cp[...], jnp.concatenate([z[0, at], z[0, at + 1]], axis=1), preferred_element_type=f32)
                    zq = [z[1:4, at + n].reshape(3 * tile, tile) for n in range(2)]
                    q = jnp.dot(cq[...], jnp.concatenate(zq, axis=1), preferred_element_type=f32)
                    for n in range(2):
                        j = at + n
                        pj, qj = p[:, n * tile : (n + 1) * tile], q[:, n * tile : (n + 1) * tile]
                        if last:
                            pj, qj = pj + vacc[1, j].astype(f32), qj + vacc[0, j].astype(f32)
                            near_j = jnp.where(u_near, qj, pj).astype(bf16)
                            cross_j = jnp.where(u_near, pj, qj).astype(bf16)
                            out_cross[j] = cross_j
                            if out_near is not None:
                                out_near[j] = near_j
                            if out_pair is not None:
                                out_pair[j] = near_j
                                out_pair[width + j] = cross_j
                        else:
                            vacc[0, j] = pj.astype(bf16)
                            vacc[1, j] = qj.astype(bf16)
                return 0

            lax.fori_loop(0, (cuts[k + 1] - cuts[k]) // 14, close, 0)
            if not last:
                carries[2 * k].start()
                carries[2 * k + 1].start()
            elif left:
                saves[k].start()
        for c in saves if last else carries:
            c.wait()


def terms(left, step, steps, info, table, envs, tensors, small, large, acc=None, onto=None):
    tile = envs[0].shape[-1]
    width = small.shape[0] // GROUP
    last = acc is not None
    final = step + 1 == steps
    joined = len(envs) == 1
    env = pltpu.VMEM((width, tile, tile), bf16)
    total = jax.ShapeDtypeStruct((2, width, tile, tile), bf16)
    n = width * GROUP
    scratch = [
        pltpu.VMEM((tile, 3 * tile), bf16),
        pltpu.VMEM((tile, tile), bf16),
        pltpu.VMEM((tile, tile), bf16),
        pltpu.VMEM((tile, 3 * tile), bf16),
        pltpu.VMEM((4 * n, 2 * tile), bf16),
        pltpu.VMEM((4 * n, 2 * tile), bf16),
        pltpu.VMEM((4, width, tile, tile), bf16),
        pltpu.VMEM((2, width, tile, tile), bf16),
        pltpu.VMEM((4, tile, tile), bf16),
        pltpu.VMEM((4, tile, tile), bf16),
        pltpu.VMEM((n, n), bf16),
        pltpu.VMEM((2 * n, 2 * n), bf16),
        pltpu.SemaphoreType.DMA((2, 3)),
        pltpu.SemaphoreType.DMA((4,)),
    ]
    if not last:
        scratch += [pltpu.VMEM((width, tile, tile), bf16)] * 2 + [pltpu.SemaphoreType.DMA((2, 3))]
    operands = [in_vmem(b) if last else b for b in envs] + [*tensors, in_hbm(small), in_hbm(large)]
    info_shape = jax.ShapeDtypeStruct(info.shape, info.dtype)
    out_specs, out_shape = [ANY, SMEM], [total, info_shape]
    aliases = {}
    if last:
        operands.append(acc)
        out_specs, out_shape = [VMEM, SMEM], [env, info_shape]
        if final or not left:
            out_specs.insert(0, VMEM)
            out_shape.insert(0, env)
        if not final:
            out_specs.insert(0, VMEM)
            out_shape.insert(0, pltpu.VMEM((2 * width, tile, tile), bf16))
        if left:
            if onto is not None:
                operands.append(onto)
                aliases = {1 + len(operands): 0}
            out_specs.insert(0, ANY)
            out_shape.insert(0, jax.ShapeDtypeStruct((steps, 1, width, tile, tile), bf16))
            scratch.append(pltpu.SemaphoreType.DMA((3,)))

    def body(info, table, *refs):
        single = None if joined else refs[1]
        refs = (refs[0], single) + refs[1 if joined else 2 :]
        terms_body(left, last, final, onto is not None, width, tile, step, steps, info, table, *refs)

    return pl.pallas_call(
        body,
        in_specs=[SMEM, SMEM] + [VMEM if last else ANY] * len(envs) + [ANY] * (len(operands) - len(envs)),
        out_specs=out_specs,
        out_shape=out_shape,
        scratch_shapes=scratch,
        input_output_aliases=aliases,
        compiler_params=pltpu.CompilerParams(vmem_limit_bytes=LIMIT),
    )(info, table, *operands)


def place_body(groups, count, direct, info, *refs):
    pieces = 3
    total = sum(len(sources) for _, _, sources in groups)
    sources, outs, held, sem = refs[:total], refs[-2 - count : -2], refs[-2], refs[-1]
    jobs = []
    for n, (out, index, flags) in enumerate(groups):
        dst = outs[out] if index is None else outs[out].at[index, 0]
        for flag in flags:
            src = sources[len(jobs)]
            cuts = [src.shape[0] * k // pieces for k in range(pieces + 1)]
            spans = [pl.ds(a, b - a) for a, b in zip(cuts, cuts[1:])]
            here = held.at[n]
            reads = [pltpu.make_async_copy(src.at[c], here.at[c], sem.at[0, n, k]) for k, c in enumerate(spans)]
            writes = [pltpu.make_async_copy(here.at[c], dst.at[c], sem.at[1, n, k]) for k, c in enumerate(spans)]
            if direct[len(jobs)]:
                reads, writes = [pltpu.make_async_copy(src.at[c], dst.at[c], sem.at[1, n, k]) for k, c in enumerate(spans)], None
            jobs.append((flag, reads, writes))

    for flag, reads, _ in jobs:

        @pl.when(flag(info))
        def _(reads=reads):
            for c in reads:
                c.start()

    for flag, reads, writes in jobs:

        @pl.when(flag(info))
        def _(reads=reads, writes=writes):
            for a, b in zip(reads, writes or ()):
                a.wait()
                b.start()

    for flag, reads, writes in jobs:

        @pl.when(flag(info))
        def _(reads=reads, writes=writes):
            for c in writes or reads:
                c.wait()


def place(info, groups, shapes, onto, resident=()):
    sources = [b for _, _, pairs in groups for _, b in pairs]
    specs = [VMEM if any(b is r for r in resident) else ANY for b in sources]
    sources = [in_vmem(b) if spec is VMEM else b for b, spec in zip(sources, specs)]
    plan = [(out, index, [flag for flag, _ in pairs]) for out, index, pairs in groups]
    return pl.pallas_call(
        functools.partial(place_body, plan, len(shapes), [spec is VMEM for spec in specs]),
        in_specs=[SMEM] + specs + [ANY] * len(onto),
        out_specs=[ANY] * len(shapes),
        out_shape=[jax.ShapeDtypeStruct(s, bf16) for s in shapes],
        scratch_shapes=[
            pltpu.VMEM((len(groups), *sources[0].shape), bf16),
            pltpu.SemaphoreType.DMA((2, len(groups), 3)),
        ],
        compiler_params=pltpu.CompilerParams(vmem_limit_bytes=LIMIT),
        input_output_aliases={1 + len(sources) + i: i for i in range(len(onto))},
    )(info, *sources, *onto)


def compact(mpo):
    sites, width = mpo.shape[:2]
    return jnp.transpose(mpo, (0, 3, 2, 4, 1)).reshape(sites, 4 * width, 4 * width)


def shards(site_tensors, mpo, left_in, right_in, tile_rows):
    chains, sectors = lax.axis_size("chain"), lax.axis_size("sector")
    routes = Routes(chains, sectors)
    chain, sector = lax.axis_index("chain"), lax.axis_index("sector")
    core, x = chain % 2, sector % 2
    sites, _, tile = site_tensors.shape[:3]
    same = core == x
    info = jnp.stack([(chain - core + x) * sites, sector // 2, x, same.astype(jnp.int32), chain]).astype(jnp.int32)

    left_near, right_own = left_in[0, 0], right_in[0, 0]
    width = left_near.shape[0]
    tensors = jnp.transpose(site_tensors[:, 0], (0, 2, 1, 3)).reshape(sites * 4, tile, tile)
    packed = jnp.concatenate([left_near, tensors])
    left_cross = move(packed, routes.left_cross)
    left_second, right_own, tensors, packed = lax.optimization_barrier((left_near, right_own, tensors, packed))
    left_near_below = move(left_second, routes.left_up)
    right_near_above = move(right_own, routes.right_native_down)
    right_near = move(right_own, routes.to_right_core)
    tensors_below = move(tensors, routes.left_up)
    tensors_right = move(tensors, routes.to_right_core)
    k = compact(mpo)
    ks = spread(info, k, move(k, routes.to_right_core))
    right_own, right_near, ks = lax.optimization_barrier((right_own, right_near, ks))
    right_cross = move(right_own, routes.right_cross)
    left_cross, left_near_below, right_near_above, ks, tensors_below, tensors_right = lax.optimization_barrier(
        (left_cross, left_near_below, right_near_above, ks, tensors_below, tensors_right)
    )
    left_cross_below = move(left_cross, routes.left_up)
    tensors_cross_right = move(left_cross[width:], routes.to_right_core)
    right_cross, tensors_cross_right = lax.optimization_barrier((right_cross, tensors_cross_right))
    right_cross_above = move(right_cross, routes.right_down)
    pair, pair_below = (tensors, left_cross), (tensors_below, left_cross_below)
    pair_right = (tensors_right, tensors_cross_right)

    l_far, r_far = (left_near_below, left_cross_below), (right_near_above, right_cross_above)
    l, r = (left_near, left_cross), (right_near, right_cross)

    def local(left, step, info, envs, tensors):
        return terms(left, step, sites, info, tile_rows, envs, tensors, ks[3 * step], ks[3 * step + 1])

    def remote(left, step, info, envs, tensors, acc, onto=None):
        return terms(left, step, sites, info, tile_rows, envs, tensors, ks[3 * step + 2], ks[3 * step + 1], acc, onto)

    envs_shape = (sites, 1, width, tile, tile)

    def own(info):
        return info[3] == 1

    def other(info):
        return info[3] != 1

    left_envs = right_envs = None
    kept = []
    l_acc, info = local(True, 0, info, l, pair)
    for step in range(sites):
        more = step + 1 < sites
        if step > 0:
            kept.append((step, left_back, list(right_back)))
        left_envs, l_first, l_cross, info = remote(True, step, info, l_far, pair_below, l_acc, left_envs)
        left_back = move(l_cross, routes.left_back)
        if more:
            l_far = [move(l_first, routes.left_up)]
            l_acc, info = local(True, step + 1, info, [l_first], pair)
        if step == 0:
            r_acc, info = local(False, step, info, r, pair_right)
        if step > 0:
            info, *kept[-1][2][:] = lax.optimization_barrier((info, *kept[-1][2]))
        *r_pair, r_near, r_cross, info = remote(False, step, info, r_far, pair_right, r_acc)
        if more:
            r_far = [move(r_pair[0], routes.right_down)]
            info, left_back = lax.optimization_barrier((info, left_back))
        right_back = (move(r_near, routes.from_right_core), move(r_cross, routes.right_back))
        if more:
            r_acc, info = local(False, step + 1, info, r_pair, pair_right)
    info, left_back = lax.optimization_barrier((info, left_back))
    for step, back, backs in kept:
        left_envs, right_envs = place(
            info,
            [(0, step - 1, [(other, back)]), (1, sites - step, list(zip((own, other), backs)))],
            [envs_shape] * 2,
            [left_envs] + ([] if right_envs is None else [right_envs]),
        )

    edge_near, edge_cross = move(l_first, routes.edge_same), move(left_back, routes.edge_other)
    edge = [
        (lambda info: info[4] == 0, left_in[0, 0]),
        (lambda info: (info[4] != 0) & (info[3] == 1), edge_cross),
        (lambda info: (info[4] != 0) & (info[3] != 1), edge_near),
    ]
    left_envs, right_envs, left_edge = place(
        info,
        [(0, sites - 1, [(other, left_back)]), (1, 0, list(zip((own, other), right_back))), (2, None, edge)],
        [envs_shape, envs_shape, (width, tile, tile)],
        [left_envs] + ([] if right_envs is None else [right_envs]),
        [left_back, *right_back, edge_cross, edge_near],
    )
    return left_envs, right_envs, left_edge[None, None]


def solution(mesh):
    placed = (
        P("chain", "sector", None, None, None),
        P("chain", None, None, None, None),
        P("chain", "sector", None, None, None),
        P("chain", "sector", None, None, None),
        P(),
    )
    return jax.shard_map(
        shards,
        mesh=mesh,
        in_specs=placed,
        out_specs=(
            P("chain", "sector", None, None, None),
            P("chain", "sector", None, None, None),
            P("chain", "sector", None, None, None),
        ),
        check_vma=False,
    )
```

```python
import functools

import jax
import jax.numpy as jnp
from jax import lax
from jax.experimental import pallas as pl
from jax.experimental.pallas import tpu as pltpu
from jax.sharding import PartitionSpec as P

f32 = jnp.float32
bf16 = jnp.bfloat16
AXES = ("chain", "sector")
SUBLANES = 8
GROUP = SUBLANES // 2
STEP_ROWS = 2 * SUBLANES
ANY = pl.BlockSpec(memory_space=pl.ANY)
SMEM = pl.BlockSpec(memory_space=pltpu.SMEM)
VMEM = pl.BlockSpec(memory_space=pltpu.VMEM)
LIMIT = 18 * 2**20


class Routes:
    def __init__(self, chains, sectors):
        def at(pair, core, z, x):
            return (2 * pair + core) * sectors + 2 * z + x

        pairs, zs = range(chains // 2), range(sectors // 2)
        every = [(y, z, e) for y in pairs for z in zs for e in (0, 1)]
        below = [(y, z, e) for y, z, e in every if z + 1 in zs]
        self.left_cross = [(at(y, e, z, 1 - e), at(y, e, z, e)) for y, z, e in every]
        self.right_cross = [(at(y, e, z, 1 - e), at(y, 1 - e, z, e)) for y, z, e in every]
        self.to_right_core = [(at(y, e, z, e), at(y, 1 - e, z, e)) for y, z, e in every]
        self.left_up = [(at(y, e, z, e), at(y, e, z + 1, e)) for y, z, e in below]
        self.right_down = [(at(y, 1 - e, z + 1, e), at(y, 1 - e, z, e)) for y, z, e in below]
        self.right_native_down = [(at(y, e, z + 1, e), at(y, 1 - e, z, e)) for y, z, e in below]
        self.left_back = [(b, a) for a, b in self.left_cross]
        self.right_back = [(b, a) for a, b in self.right_cross]
        self.from_right_core = [(b, a) for a, b in self.to_right_core]
        shifts = [(c, q) for c in range(chains - 1) for q in range(sectors)]
        self.edge_same = [(c * sectors + q, (c + 1) * sectors + q) for c, q in shifts if c % 2 == q % 2]
        self.edge_other = [(c * sectors + q, (c + 1) * sectors + q) for c, q in shifts if c % 2 != q % 2]


def move(block, route):
    return lax.ppermute(block, AXES, route)


def in_hbm(x):
    return pltpu.with_memory_space_constraint(x, pltpu.HBM)


def in_vmem(x):
    return pltpu.with_memory_space_constraint(x, pltpu.VMEM)


def spread_body(width, steps, info, own, received, *outs):
    def spread(k, states, flip):
        n = len(states) * width * GROUP
        cols = 4 * width
        row = lax.broadcasted_iota(jnp.int32, (n, cols), 0) // GROUP
        col = lax.broadcasted_iota(jnp.int32, (n, cols), 1)
        pick = jnp.where(row + states[0] * width == col, 1.0, 0.0)
        if not flip:
            mid = jnp.dot(pick.astype(bf16), k, preferred_element_type=f32).astype(bf16)
            out = lax.dot_general(
                mid, pick.astype(bf16), (((1,), (1,)), ((), ())), preferred_element_type=f32
            )
        else:
            out = jnp.zeros((n, n), f32)
            group = lax.broadcasted_iota(jnp.int32, (n, width), 0) // GROUP
            inner = lax.broadcasted_iota(jnp.int32, (n, width), 1)
            tall = [jnp.where(group - i * width == inner, 1.0, 0.0).astype(bf16) for i in range(len(states))]
            for i, a in enumerate(states):
                for j, b in enumerate(states):
                    block = k[a * width : (a + 1) * width, b * width : (b + 1) * width]
                    mid = lax.dot_general(
                        tall[i], block, (((1,), (1,)), ((), ())), preferred_element_type=f32
                    ).astype(bf16)
                    out += lax.dot_general(
                        mid, tall[j], (((1,), (1,)), ((), ())), preferred_element_type=f32
                    )
        i = lax.broadcasted_iota(jnp.int32, out.shape, 0) % GROUP
        j = lax.broadcasted_iota(jnp.int32, out.shape, 1) % GROUP
        return jnp.where(i == j, out, 0.0).astype(bf16)

    def fill(source, flip):
        for step in range(steps):
            k = source[steps - 1 - step if flip else step]
            for i, states in enumerate(((0,), (1, 2), (3,))):
                outs[3 * step + i][...] = spread(k, states, flip)

    @pl.when(info[3] == 1)
    def _():
        fill(own, False)

    @pl.when(info[3] != 1)
    def _():
        fill(received, True)


def spread(info, own, received):
    steps, width = own.shape[0], own.shape[1] // 4
    n = width * GROUP
    shapes = [(n, n), (2 * n, 2 * n), (n, n)] * steps
    return pl.pallas_call(
        functools.partial(spread_body, width, steps),
        in_specs=[SMEM, VMEM, VMEM],
        out_specs=[VMEM] * len(shapes),
        out_shape=[pltpu.HBM(s, bf16) for s in shapes],
        compiler_params=pltpu.CompilerParams(vmem_limit_bytes=LIMIT),
    )(info, own, received)


def terms_body(left, last, final, onto, width, tile, step, steps, info, table, pair, pieces, a_near, a_cross, small, large, *rest):
    joined = not pieces
    if last:
        acc, *rest = rest
        if left:
            rest = rest[1:] if onto else rest
            envs, *rest = rest
            *rest, envs_sem = rest
        out_pair = out_near = None
        if not final:
            out_pair, *rest = rest
        if final or not left:
            out_near, *rest = rest
        out_cross, info_out, *rest = rest
    else:
        acc, info_out, *rest = rest
    bd, bm, cp, cq, one0, two0, one1, two1, z, vacc, an, ac, ks, kd, sem, weight_sem, *rest = rest
    first, zpos, x, same = info[0], info[1], info[2], info[3]
    for i in range(info.shape[0]):
        info_out[i] = info[i]
    active = same if left else 1 - same
    u_near = (x == 0) if left else (x == 1)
    cuts = [0, width // 6 * 2, width // 6 * 4, width]
    site = step if left else steps - 1 - step

    def carry(which, k):
        c = pl.ds(cuts[k], cuts[k + 1] - cuts[k])
        ends = (acc.at[which, c], vacc.at[which, c])
        return pltpu.make_async_copy(*(ends if last else ends[::-1]), sem.at[which, k])

    def save(k):
        c = pl.ds(cuts[k], cuts[k + 1] - cuts[k])
        return pltpu.make_async_copy((out_pair if out_near is None else out_near).at[c], envs.at[step, 0, c], envs_sem.at[k])

    carries = [carry(which, k) for k in range(3) for which in range(2)]
    saves = [save(k) for k in range(3)] if last and left else []
    factors = [
        pltpu.make_async_copy(src.at[pl.ds(src.shape[0] - 4 * (steps - site), 4)], dst, weight_sem.at[i])
        for i, (src, dst) in enumerate(((a_near, an), (a_cross, ac)))
    ]
    weights = [
        pltpu.make_async_copy(src, dst, weight_sem.at[2 + i]) for i, (src, dst) in enumerate(((small, ks), (large, kd)))
    ]
    fetches = []
    share = width // max(len(pieces), 1)
    if rest:
        near, cross, fetch_sem = rest
        for k in range(3):
            c = pl.ds(cuts[k], cuts[k + 1] - cuts[k])
            fetches.append(pltpu.make_async_copy(pair.at[c], near.at[c], fetch_sem.at[0, k]))
            if joined or len(pieces) == 1:
                src = pair.at[pl.ds(width + cuts[k], cuts[k + 1] - cuts[k])] if joined else pieces[0].at[c]
                fetches.append(pltpu.make_async_copy(src, cross.at[c], fetch_sem.at[1, k]))
        if len(pieces) > 1:
            for k, src in enumerate(pieces):
                dst = cross.at[pl.ds(k * share, share)]
                fetches.append(pltpu.make_async_copy(src, dst, fetch_sem.at[1, k]))
        crosses = [cross]
    elif joined:
        near, crosses = pair.at[pl.ds(0, width)], [pair.at[pl.ds(width, width)]]
    else:
        near, crosses = pair, [piece.at[pl.ds(0, share)] for piece in pieces]

    @pl.when(active == 1)
    def _():
        for c in factors + fetches + weights + (carries if last else []):
            c.start()
        count = table.shape[1]
        source_bond = first + (site if left else site + 1)
        target_bond = first + (site + 1 if left else site)
        sign = 1 if left else -1
        u = 2 * zpos if left else 2 * zpos + 1
        v = u + sign
        far_u, far_v = u - 2 * sign, v - 2 * sign

        def rows_of(bond, index):
            safe = jnp.clip(index, 0, count - 1)
            return jnp.where((index >= 0) & (index < count), table[bond, safe], 0)

        sub = lax.broadcasted_iota(jnp.int32, (tile, tile), 0)
        lane = lax.broadcasted_iota(jnp.int32, (tile, tile), 1)

        def factor(of_u, state, source, target):
            a = jnp.where(u_near if of_u else jnp.logical_not(u_near), an[state].astype(f32), ac[state].astype(f32))
            a = a if left else a.T
            keep = (sub < rows_of(source_bond, source)) & (lane < rows_of(target_bond, target))
            return jnp.where(keep, a, 0.0)

        for c in factors:
            c.wait()
        if last:
            dual = [factor(False, 3, far_v, v)] + [factor(not left, t, far_v, u) for t in (1, 2)]
            mono = factor(True, 3, far_u, u)
        else:
            dual = [factor(True, 0, u, u)] + [factor(left, t, u, v) for t in (1, 2)]
            mono = factor(False, 0, v, v)
        for i, m in enumerate(dual):
            bd[:, i * tile : (i + 1) * tile] = m.astype(bf16)
        bm[...] = mono.astype(bf16)
        cp[...] = dual[0].T.astype(bf16)
        for i, m in enumerate((dual[1], dual[2], mono)):
            cq[:, i * tile : (i + 1) * tile] = m.T.astype(bf16)

        dual_near = jnp.logical_not(u_near) if last else u_near

        for f in fetches:
            f.wait()
        n = width * GROUP

        def exchange(a, b):
            upper = lax.broadcasted_iota(jnp.int32, a.shape, 1) < GROUP
            return (
                jnp.where(upper, a, pltpu.roll(b, GROUP, 1)),
                jnp.where(upper, pltpu.roll(a, GROUP, 1), b),
            )

        def split(part):
            pairs = part.reshape(width // 2, 2, SUBLANES, tile)
            return jnp.concatenate([h.reshape(n, tile) for h in exchange(pairs[:, 0], pairs[:, 1])], axis=1)

        def joined_rows(part):
            part = part.reshape(width // 2, SUBLANES, 2 * tile)
            a, b = exchange(part[..., :tile], part[..., tile:])
            return jnp.stack([a, b], axis=1).reshape(width, SUBLANES, tile)

        def products(i, slots):
            one, two = slots
            r = pl.ds(pl.multiple_of(i * STEP_ROWS, STEP_ROWS), STEP_ROWS)
            e_n = near[:, r, :]
            e_c = jnp.concatenate([c[:, r, :] for c in crosses], axis=0)
            e_d = jnp.where(dual_near, e_n, e_c).reshape(width * STEP_ROWS, tile)
            e_m = jnp.where(dual_near, e_c, e_n).reshape(width * STEP_ROWS, tile)
            yd = jnp.dot(e_d, bd[...], preferred_element_type=f32).reshape(width, STEP_ROWS, 3 * tile)
            ym = jnp.dot(e_m, bm[...], preferred_element_type=f32).reshape(width, STEP_ROWS, tile)
            for h in range(2):
                c = slice(h * SUBLANES, (h + 1) * SUBLANES)
                one[2 * h] = split(yd[:, c, :tile]).astype(bf16)
                one[2 * h + 1] = split(ym[:, c, :]).astype(bf16)
                two[h] = jnp.concatenate(
                    [split(yd[:, c, t * tile : (t + 1) * tile]) for t in (1, 2)], axis=0
                ).astype(bf16)

        def mix(i, slots):
            one, two = slots
            r = pl.ds(pl.multiple_of(i * STEP_ROWS, STEP_ROWS), STEP_ROWS)

            def put(to, halves):
                z[to, :, r, :] = jnp.concatenate([joined_rows(x) for x in halves], axis=1).astype(bf16)

            for m, to in ((0, 0), (1, 3)):
                put(to, [jnp.dot(ks[...], one[2 * h + m], preferred_element_type=f32) for h in range(2)])
            mixed = [jnp.dot(kd[...], two[h], preferred_element_type=f32) for h in range(2)]
            for t in range(2):
                put(1 + t, [x[t * n : (t + 1) * n] for x in mixed])

        y0, y1 = (one0, two0), (one1, two1)
        count_rows = tile // STEP_ROWS
        products(0, y0)
        for c in weights:
            c.wait()

        def turn(j, _):
            for k in range(2 // 2):
                i = 2 * j + 2 * k
                products(i + 1, y1)
                mix(i, y0)
                products(jnp.minimum(i + 2, count_rows - 2), y0)
                mix(i + 1, y1)
            return 0

        lax.fori_loop(0, count_rows // 2, turn, 0)
        if last:
            for c in carries:
                c.wait()
        for k in range(3):
            def close(m, _, k=k):
                for i in range(7):
                    at = cuts[k] + 2 * (m * 7 + i)
                    p = jnp.dot(cp[...], jnp.concatenate([z[0, at], z[0, at + 1]], axis=1), preferred_element_type=f32)
                    zq = [z[1:4, at + n].reshape(3 * tile, tile) for n in range(2)]
                    q = jnp.dot(cq[...], jnp.concatenate(zq, axis=1), preferred_element_type=f32)
                    for n in range(2):
                        j = at + n
                        pj, qj = p[:, n * tile : (n + 1) * tile], q[:, n * tile : (n + 1) * tile]
                        if last:
                            pj, qj = pj + vacc[1, j].astype(f32), qj + vacc[0, j].astype(f32)
                            near_j = jnp.where(u_near, qj, pj).astype(bf16)
                            cross_j = jnp.where(u_near, pj, qj).astype(bf16)
                            out_cross[j] = cross_j
                            if out_near is not None:
                                out_near[j] = near_j
                            if out_pair is not None:
                                out_pair[j] = near_j
                                out_pair[width + j] = cross_j
                        else:
                            vacc[0, j] = pj.astype(bf16)
                            vacc[1, j] = qj.astype(bf16)
                return 0

            lax.fori_loop(0, (cuts[k + 1] - cuts[k]) // 14, close, 0)
            if not last:
                carries[2 * k].start()
                carries[2 * k + 1].start()
            elif left:
                saves[k].start()
        for c in saves if last else carries:
            c.wait()


def terms(left, step, steps, info, table, envs, tensors, small, large, acc=None, onto=None):
    tile = envs[0].shape[-1]
    width = small.shape[0] // GROUP
    last = acc is not None
    final = step + 1 == steps
    pieces = len(envs) - 1
    env = pltpu.VMEM((width, tile, tile), bf16)
    total = jax.ShapeDtypeStruct((2, width, tile, tile), bf16)
    n = width * GROUP
    scratch = [
        pltpu.VMEM((tile, 3 * tile), bf16),
        pltpu.VMEM((tile, tile), bf16),
        pltpu.VMEM((tile, tile), bf16),
        pltpu.VMEM((tile, 3 * tile), bf16),
        *[pltpu.VMEM(shape, bf16) for _ in range(2) for shape in ((4, n, 2 * tile), (2, 2 * n, 2 * tile))],
        pltpu.VMEM((4, width, tile, tile), bf16),
        pltpu.VMEM((2, width, tile, tile), bf16),
        pltpu.VMEM((4, tile, tile), bf16),
        pltpu.VMEM((4, tile, tile), bf16),
        pltpu.VMEM((n, n), bf16),
        pltpu.VMEM((2 * n, 2 * n), bf16),
        pltpu.SemaphoreType.DMA((2, 3)),
        pltpu.SemaphoreType.DMA((4,)),
    ]
    if not last:
        scratch += [pltpu.VMEM((width, tile, tile), bf16)] * 2 + [pltpu.SemaphoreType.DMA((2, 3))]
    operands = [in_vmem(b) if last else b for b in envs] + [*tensors, in_hbm(small), in_hbm(large)]
    info_shape = jax.ShapeDtypeStruct(info.shape, info.dtype)
    out_specs, out_shape = [ANY, SMEM], [total, info_shape]
    aliases = {}
    if last:
        operands.append(acc)
        out_specs, out_shape = [VMEM, SMEM], [env, info_shape]
        if final or not left:
            out_specs.insert(0, VMEM)
            out_shape.insert(0, env)
        if not final:
            out_specs.insert(0, VMEM)
            out_shape.insert(0, pltpu.VMEM((2 * width, tile, tile), bf16))
        if left:
            if onto is not None:
                operands.append(onto)
                aliases = {1 + len(operands): 0}
            out_specs.insert(0, ANY)
            out_shape.insert(0, jax.ShapeDtypeStruct((steps, 1, width, tile, tile), bf16))
            scratch.append(pltpu.SemaphoreType.DMA((3,)))

    def body(info, table, *refs):
        refs = (refs[0], refs[1 : 1 + pieces]) + refs[1 + pieces :]
        terms_body(left, last, final, onto is not None, width, tile, step, steps, info, table, *refs)

    return pl.pallas_call(
        body,
        in_specs=[SMEM, SMEM] + [VMEM if last else ANY] * len(envs) + [ANY] * (len(operands) - len(envs)),
        out_specs=out_specs,
        out_shape=out_shape,
        scratch_shapes=scratch,
        input_output_aliases=aliases,
        compiler_params=pltpu.CompilerParams(vmem_limit_bytes=LIMIT),
    )(info, table, *operands)


def place_body(groups, count, direct, info, *refs):
    pieces = 3
    total = sum(len(sources) for _, _, sources in groups)
    sources, outs, held, sem = refs[:total], refs[-2 - count : -2], refs[-2], refs[-1]
    jobs = []
    for n, (out, index, flags) in enumerate(groups):
        dst = outs[out] if index is None else outs[out].at[index, 0]
        for flag in flags:
            src = sources[len(jobs)]
            cuts = [src.shape[0] * k // pieces for k in range(pieces + 1)]
            spans = [pl.ds(a, b - a) for a, b in zip(cuts, cuts[1:])]
            here = held.at[n]
            reads = [pltpu.make_async_copy(src.at[c], here.at[c], sem.at[0, n, k]) for k, c in enumerate(spans)]
            writes = [pltpu.make_async_copy(here.at[c], dst.at[c], sem.at[1, n, k]) for k, c in enumerate(spans)]
            if direct[len(jobs)]:
                reads, writes = [pltpu.make_async_copy(src.at[c], dst.at[c], sem.at[1, n, k]) for k, c in enumerate(spans)], None
            jobs.append((flag, reads, writes))

    for flag, reads, _ in jobs:

        @pl.when(flag(info))
        def _(reads=reads):
            for c in reads:
                c.start()

    for flag, reads, writes in jobs:

        @pl.when(flag(info))
        def _(reads=reads, writes=writes):
            for a, b in zip(reads, writes or ()):
                a.wait()
                b.start()

    for flag, reads, writes in jobs:

        @pl.when(flag(info))
        def _(reads=reads, writes=writes):
            for c in writes or reads:
                c.wait()


def place(info, groups, shapes, onto, resident=()):
    sources = [b for _, _, pairs in groups for _, b in pairs]
    specs = [VMEM if any(b is r for r in resident) else ANY for b in sources]
    sources = [in_vmem(b) if spec is VMEM else b for b, spec in zip(sources, specs)]
    plan = [(out, index, [flag for flag, _ in pairs]) for out, index, pairs in groups]
    return pl.pallas_call(
        functools.partial(place_body, plan, len(shapes), [spec is VMEM for spec in specs]),
        in_specs=[SMEM] + specs + [ANY] * len(onto),
        out_specs=[ANY] * len(shapes),
        out_shape=[jax.ShapeDtypeStruct(s, bf16) for s in shapes],
        scratch_shapes=[
            pltpu.VMEM((len(groups), *sources[0].shape), bf16),
            pltpu.SemaphoreType.DMA((2, len(groups), 3)),
        ],
        compiler_params=pltpu.CompilerParams(vmem_limit_bytes=LIMIT),
        input_output_aliases={1 + len(sources) + i: i for i in range(len(onto))},
    )(info, *sources, *onto)


def compact(mpo):
    sites, width = mpo.shape[:2]
    return jnp.transpose(mpo, (0, 3, 2, 4, 1)).reshape(sites, 4 * width, 4 * width)


def shards(site_tensors, mpo, left_in, right_in, tile_rows):
    chains, sectors = lax.axis_size("chain"), lax.axis_size("sector")
    routes = Routes(chains, sectors)
    chain, sector = lax.axis_index("chain"), lax.axis_index("sector")
    core, x = chain % 2, sector % 2
    sites, _, tile = site_tensors.shape[:3]
    same = core == x
    info = jnp.stack([(chain - core + x) * sites, sector // 2, x, same.astype(jnp.int32), chain]).astype(jnp.int32)

    left_near, right_own = left_in[0, 0], right_in[0, 0]
    width = left_near.shape[0]
    tensors = jnp.transpose(site_tensors[:, 0], (0, 2, 1, 3)).reshape(sites * 4, tile, tile)
    packed = jnp.concatenate([left_near, tensors])
    left_cross = move(packed, routes.left_cross)
    left_second, right_own, tensors, packed = lax.optimization_barrier((left_near, right_own, tensors, packed))
    left_near_below = move(left_second, routes.left_up)
    right_near_above = move(right_own, routes.right_native_down)
    right_near = move(right_own, routes.to_right_core)
    tensors_below = move(tensors, routes.left_up)
    tensors_right = move(tensors, routes.to_right_core)
    k = compact(mpo)
    k_right = move(k, routes.to_right_core)
    right_own, k_right = lax.optimization_barrier((right_own, k_right))
    cuts = [0, width // 2, width] if width % 2 == 0 else [0, width]
    right_cross = [move(right_own[a:b], routes.right_cross) for a, b in zip(cuts, cuts[1:])]
    ks = spread(info, k, k_right)
    left_cross, left_near_below, right_near_above, ks, tensors_below, tensors_right = lax.optimization_barrier(
        (left_cross, left_near_below, right_near_above, ks, tensors_below, tensors_right)
    )
    left_cross_below = move(left_cross, routes.left_up)
    tensors_cross_right = move(left_cross[width:], routes.to_right_core)
    right_cross_above = [move(b, routes.right_down) for b in right_cross]
    pair, pair_below = (tensors, left_cross), (tensors_below, left_cross_below)
    pair_right = (tensors_right, tensors_cross_right)

    l_far, r_far = (left_near_below, left_cross_below), (right_near_above, *right_cross_above)
    l, r = (in_hbm(left_near), left_cross), (right_near, *right_cross)

    def local(left, step, info, envs, tensors):
        return terms(left, step, sites, info, tile_rows, envs, tensors, ks[3 * step], ks[3 * step + 1])

    def remote(left, step, info, envs, tensors, acc, onto=None):
        return terms(left, step, sites, info, tile_rows, envs, tensors, ks[3 * step + 2], ks[3 * step + 1], acc, onto)

    envs_shape = (sites, 1, width, tile, tile)

    def own(info):
        return info[3] == 1

    def other(info):
        return info[3] != 1

    left_envs = right_envs = None
    kept = []
    info, tensors_cross_right = lax.optimization_barrier((info, tensors_cross_right))
    pair_right = (tensors_right, tensors_cross_right)
    l_acc, info = local(True, 0, info, l, pair)
    for step in range(sites):
        more = step + 1 < sites
        if step > 0:
            kept.append((step, left_back, list(right_back)))
        left_envs, l_first, l_cross, info = remote(True, step, info, l_far, pair_below, l_acc, left_envs)
        left_back = move(l_cross, routes.left_back)
        if more:
            l_far = [move(l_first, routes.left_up)]
            l_acc, info = local(True, step + 1, info, [l_first], pair)
        if step == 0:
            r_acc, info = local(False, step, info, r, pair_right)
        if step > 0:
            info, *kept[-1][2][:] = lax.optimization_barrier((info, *kept[-1][2]))
        *r_pair, r_near, r_cross, info = remote(False, step, info, r_far, pair_right, r_acc)
        if more:
            r_far = [move(r_pair[0], routes.right_down)]
            info, left_back = lax.optimization_barrier((info, left_back))
        right_back = (move(r_near, routes.from_right_core), move(r_cross, routes.right_back))
        if more:
            r_acc, info = local(False, step + 1, info, r_pair, pair_right)
    info, left_back = lax.optimization_barrier((info, left_back))
    for step, back, backs in kept:
        left_envs, right_envs = place(
            info,
            [(0, step - 1, [(other, back)]), (1, sites - step, list(zip((own, other), backs)))],
            [envs_shape] * 2,
            [left_envs] + ([] if right_envs is None else [right_envs]),
        )

    edge_tile = move(jnp.where(same, l_first, left_back), routes.edge_same + routes.edge_other)
    edge = [
        (lambda info: info[4] == 0, left_in[0, 0]),
        (lambda info: info[4] != 0, edge_tile),
    ]
    left_envs, right_envs, left_edge = place(
        info,
        [(0, sites - 1, [(other, left_back)]), (1, 0, list(zip((own, other), right_back))), (2, None, edge)],
        [envs_shape, envs_shape, (width, tile, tile)],
        [left_envs] + ([] if right_envs is None else [right_envs]),
        [left_back, *right_back, edge_tile],
    )
    return left_envs, right_envs, left_edge[None, None]


def solution(mesh):
    placed = (
        P("chain", "sector", None, None, None),
        P("chain", None, None, None, None),
        P("chain", "sector", None, None, None),
        P("chain", "sector", None, None, None),
        P(),
    )
    return jax.shard_map(
        shards,
        mesh=mesh,
        in_specs=placed,
        out_specs=(
            P("chain", "sector", None, None, None),
            P("chain", "sector", None, None, None),
            P("chain", "sector", None, None, None),
        ),
        check_vma=False,
    )
```

```python
import functools

import jax
import jax.numpy as jnp
from jax import lax
from jax.experimental import pallas as pl
from jax.experimental.pallas import tpu as pltpu
from jax.sharding import PartitionSpec as P

f32 = jnp.float32
bf16 = jnp.bfloat16
AXES = ("chain", "sector")
SUBLANES = 8
GROUP = SUBLANES // 2
STEP_ROWS = 2 * SUBLANES
ANY = pl.BlockSpec(memory_space=pl.ANY)
SMEM = pl.BlockSpec(memory_space=pltpu.SMEM)
VMEM = pl.BlockSpec(memory_space=pltpu.VMEM)
LIMIT = 18 * 2**20


class Routes:
    def __init__(self, chains, sectors):
        def at(pair, core, z, x):
            return (2 * pair + core) * sectors + 2 * z + x

        pairs, zs = range(chains // 2), range(sectors // 2)
        every = [(y, z, e) for y in pairs for z in zs for e in (0, 1)]
        below = [(y, z, e) for y, z, e in every if z + 1 in zs]
        self.left_cross = [(at(y, e, z, 1 - e), at(y, e, z, e)) for y, z, e in every]
        self.right_cross = [(at(y, e, z, 1 - e), at(y, 1 - e, z, e)) for y, z, e in every]
        self.to_right_core = [(at(y, e, z, e), at(y, 1 - e, z, e)) for y, z, e in every]
        self.left_up = [(at(y, e, z, e), at(y, e, z + 1, e)) for y, z, e in below]
        self.right_down = [(at(y, 1 - e, z + 1, e), at(y, 1 - e, z, e)) for y, z, e in below]
        self.right_native_down = [(at(y, e, z + 1, e), at(y, 1 - e, z, e)) for y, z, e in below]
        self.left_back = [(b, a) for a, b in self.left_cross]
        self.right_back = [(b, a) for a, b in self.right_cross]
        self.from_right_core = [(b, a) for a, b in self.to_right_core]
        shifts = [(c, q) for c in range(chains - 1) for q in range(sectors)]
        self.edge_same = [(c * sectors + q, (c + 1) * sectors + q) for c, q in shifts if c % 2 == q % 2]
        self.edge_other = [(c * sectors + q, (c + 1) * sectors + q) for c, q in shifts if c % 2 != q % 2]


def move(block, route):
    return lax.ppermute(block, AXES, route)


def in_hbm(x):
    return pltpu.with_memory_space_constraint(x, pltpu.HBM)


def in_vmem(x):
    return pltpu.with_memory_space_constraint(x, pltpu.VMEM)


def spread_body(width, steps, info, own, received, *outs):
    def spread(k, states, flip):
        n = len(states) * width * GROUP
        cols = 4 * width
        row = lax.broadcasted_iota(jnp.int32, (n, cols), 0) // GROUP
        col = lax.broadcasted_iota(jnp.int32, (n, cols), 1)
        pick = jnp.where(row + states[0] * width == col, 1.0, 0.0)
        if not flip:
            mid = jnp.dot(pick.astype(bf16), k, preferred_element_type=f32).astype(bf16)
            out = lax.dot_general(
                mid, pick.astype(bf16), (((1,), (1,)), ((), ())), preferred_element_type=f32
            )
        else:
            out = jnp.zeros((n, n), f32)
            group = lax.broadcasted_iota(jnp.int32, (n, width), 0) // GROUP
            inner = lax.broadcasted_iota(jnp.int32, (n, width), 1)
            tall = [jnp.where(group - i * width == inner, 1.0, 0.0).astype(bf16) for i in range(len(states))]
            for i, a in enumerate(states):
                for j, b in enumerate(states):
                    block = k[a * width : (a + 1) * width, b * width : (b + 1) * width]
                    mid = lax.dot_general(
                        tall[i], block, (((1,), (1,)), ((), ())), preferred_element_type=f32
                    ).astype(bf16)
                    out += lax.dot_general(
                        mid, tall[j], (((1,), (1,)), ((), ())), preferred_element_type=f32
                    )
        i = lax.broadcasted_iota(jnp.int32, out.shape, 0) % GROUP
        j = lax.broadcasted_iota(jnp.int32, out.shape, 1) % GROUP
        return jnp.where(i == j, out, 0.0).astype(bf16)

    def fill(source, flip):
        for step in range(steps):
            k = source[steps - 1 - step if flip else step]
            for i, states in enumerate(((0,), (1, 2), (3,))):
                outs[3 * step + i][...] = spread(k, states, flip)

    @pl.when(info[3] == 1)
    def _():
        fill(own, False)

    @pl.when(info[3] != 1)
    def _():
        fill(received, True)


def spread(info, own, received):
    steps, width = own.shape[0], own.shape[1] // 4
    n = width * GROUP
    shapes = [(n, n), (2 * n, 2 * n), (n, n)] * steps
    return pl.pallas_call(
        functools.partial(spread_body, width, steps),
        in_specs=[SMEM, VMEM, VMEM],
        out_specs=[VMEM] * len(shapes),
        out_shape=[pltpu.HBM(s, bf16) for s in shapes],
        compiler_params=pltpu.CompilerParams(vmem_limit_bytes=LIMIT),
    )(info, own, received)


def terms_body(left, last, final, onto, width, tile, step, steps, info, table, pair, pieces, a_near, a_cross, small, large, *rest):
    joined = not pieces
    if last:
        acc, *rest = rest
        if left:
            rest = rest[1:] if onto else rest
            envs, *rest = rest
            *rest, envs_sem = rest
        out_pair = out_near = None
        if not final:
            out_pair, *rest = rest
        if final or not left:
            out_near, *rest = rest
        out_cross, info_out, *rest = rest
    else:
        acc, info_out, *rest = rest
    bd, bm, cp, cq, one0, two0, one1, two1, z, vacc, an, ac, ks, kd, sem, weight_sem, *rest = rest
    first, zpos, x, same = info[0], info[1], info[2], info[3]
    for i in range(info.shape[0]):
        info_out[i] = info[i]
    active = same if left else 1 - same
    u_near = (x == 0) if left else (x == 1)
    cuts = [0, width // 6 * 2, width // 6 * 4, width]
    site = step if left else steps - 1 - step

    def carry(which, k):
        c = pl.ds(cuts[k], cuts[k + 1] - cuts[k])
        ends = (acc.at[which, c], vacc.at[which, c])
        return pltpu.make_async_copy(*(ends if last else ends[::-1]), sem.at[which, k])

    def save(k):
        c = pl.ds(cuts[k], cuts[k + 1] - cuts[k])
        return pltpu.make_async_copy((out_pair if out_near is None else out_near).at[c], envs.at[step, 0, c], envs_sem.at[k])

    carries = [carry(which, k) for k in range(3) for which in range(2)]
    saves = [save(k) for k in range(3)] if last and left else []
    factors = [
        pltpu.make_async_copy(src.at[pl.ds(src.shape[0] - 4 * (steps - site), 4)], dst, weight_sem.at[i])
        for i, (src, dst) in enumerate(((a_near, an), (a_cross, ac)))
    ]
    weights = [
        pltpu.make_async_copy(src, dst, weight_sem.at[2 + i]) for i, (src, dst) in enumerate(((small, ks), (large, kd)))
    ]
    fetches = []
    share = width // max(len(pieces), 1)
    if rest:
        near, cross, fetch_sem = rest
        for k in range(3):
            c = pl.ds(cuts[k], cuts[k + 1] - cuts[k])
            fetches.append(pltpu.make_async_copy(pair.at[c], near.at[c], fetch_sem.at[0, k]))
            if joined or len(pieces) == 1:
                src = pair.at[pl.ds(width + cuts[k], cuts[k + 1] - cuts[k])] if joined else pieces[0].at[c]
                fetches.append(pltpu.make_async_copy(src, cross.at[c], fetch_sem.at[1, k]))
        if len(pieces) > 1:
            for k, src in enumerate(pieces):
                dst = cross.at[pl.ds(k * share, share)]
                fetches.append(pltpu.make_async_copy(src, dst, fetch_sem.at[1, k]))
        crosses = [cross]
    elif joined:
        near, crosses = pair.at[pl.ds(0, width)], [pair.at[pl.ds(width, width)]]
    else:
        near, crosses = pair, [piece.at[pl.ds(0, share)] for piece in pieces]

    @pl.when(active == 1)
    def _():
        for c in factors + fetches + weights + (carries if last else []):
            c.start()
        count = table.shape[1]
        source_bond = first + (site if left else site + 1)
        target_bond = first + (site + 1 if left else site)
        sign = 1 if left else -1
        u = 2 * zpos if left else 2 * zpos + 1
        v = u + sign
        far_u, far_v = u - 2 * sign, v - 2 * sign

        def rows_of(bond, index):
            safe = jnp.clip(index, 0, count - 1)
            return jnp.where((index >= 0) & (index < count), table[bond, safe], 0)

        sub = lax.broadcasted_iota(jnp.int32, (tile, tile), 0)
        lane = lax.broadcasted_iota(jnp.int32, (tile, tile), 1)

        def factor(of_u, state, source, target):
            a = jnp.where(u_near if of_u else jnp.logical_not(u_near), an[state].astype(f32), ac[state].astype(f32))
            a = a if left else a.T
            keep = (sub < rows_of(source_bond, source)) & (lane < rows_of(target_bond, target))
            return jnp.where(keep, a, 0.0)

        for c in factors:
            c.wait()
        if last:
            dual = [factor(False, 3, far_v, v)] + [factor(not left, t, far_v, u) for t in (1, 2)]
            mono = factor(True, 3, far_u, u)
        else:
            dual = [factor(True, 0, u, u)] + [factor(left, t, u, v) for t in (1, 2)]
            mono = factor(False, 0, v, v)
        for i, m in enumerate(dual):
            bd[:, i * tile : (i + 1) * tile] = m.astype(bf16)
        bm[...] = mono.astype(bf16)
        cp[...] = dual[0].T.astype(bf16)
        for i, m in enumerate((dual[1], dual[2], mono)):
            cq[:, i * tile : (i + 1) * tile] = m.T.astype(bf16)

        dual_near = jnp.logical_not(u_near) if last else u_near

        for f in fetches:
            f.wait()
        n = width * GROUP

        def exchange(a, b):
            upper = lax.broadcasted_iota(jnp.int32, a.shape, 1) < GROUP
            return (
                jnp.where(upper, a, pltpu.roll(b, GROUP, 1)),
                jnp.where(upper, pltpu.roll(a, GROUP, 1), b),
            )

        def split(part):
            pairs = part.reshape(width // 2, 2, SUBLANES, tile)
            return jnp.concatenate([h.reshape(n, tile) for h in exchange(pairs[:, 0], pairs[:, 1])], axis=1)

        def joined_rows(part):
            part = part.reshape(width // 2, SUBLANES, 2 * tile)
            a, b = exchange(part[..., :tile], part[..., tile:])
            return jnp.stack([a, b], axis=1).reshape(width, SUBLANES, tile)

        def products(i, slots):
            one, two = slots
            r = pl.ds(pl.multiple_of(i * STEP_ROWS, STEP_ROWS), STEP_ROWS)
            e_n = near[:, r, :]
            e_c = jnp.concatenate([c[:, r, :] for c in crosses], axis=0)
            e_d = jnp.where(dual_near, e_n, e_c).reshape(width * STEP_ROWS, tile)
            e_m = jnp.where(dual_near, e_c, e_n).reshape(width * STEP_ROWS, tile)
            yd = jnp.dot(e_d, bd[...], preferred_element_type=f32).reshape(width, STEP_ROWS, 3 * tile)
            ym = jnp.dot(e_m, bm[...], preferred_element_type=f32).reshape(width, STEP_ROWS, tile)
            for h in range(2):
                c = slice(h * SUBLANES, (h + 1) * SUBLANES)
                one[2 * h] = split(yd[:, c, :tile]).astype(bf16)
                one[2 * h + 1] = split(ym[:, c, :]).astype(bf16)
                two[h] = jnp.concatenate(
                    [split(yd[:, c, t * tile : (t + 1) * tile]) for t in (1, 2)], axis=0
                ).astype(bf16)

        def mix(i, slots):
            one, two = slots
            r = pl.ds(pl.multiple_of(i * STEP_ROWS, STEP_ROWS), STEP_ROWS)

            def put(to, halves):
                z[to, :, r, :] = jnp.concatenate([joined_rows(x) for x in halves], axis=1).astype(bf16)

            for m, to in ((0, 0), (1, 3)):
                put(to, [jnp.dot(ks[...], one[2 * h + m], preferred_element_type=f32) for h in range(2)])
            mixed = [jnp.dot(kd[...], two[h], preferred_element_type=f32) for h in range(2)]
            for t in range(2):
                put(1 + t, [x[t * n : (t + 1) * n] for x in mixed])

        y0, y1 = (one0, two0), (one1, two1)
        count_rows = tile // STEP_ROWS
        products(0, y0)
        for c in weights:
            c.wait()

        def turn(j, _):
            for k in range(2 // 2):
                i = 2 * j + 2 * k
                products(i + 1, y1)
                mix(i, y0)
                products(jnp.minimum(i + 2, count_rows - 2), y0)
                mix(i + 1, y1)
            return 0

        lax.fori_loop(0, count_rows // 2, turn, 0)
        if last:
            for c in carries:
                c.wait()
        for k in range(3):
            def close(m, _, k=k):
                for i in range(7):
                    at = cuts[k] + 2 * (m * 7 + i)
                    p = jnp.dot(cp[...], jnp.concatenate([z[0, at], z[0, at + 1]], axis=1), preferred_element_type=f32)
                    zq = [z[1:4, at + n].reshape(3 * tile, tile) for n in range(2)]
                    q = jnp.dot(cq[...], jnp.concatenate(zq, axis=1), preferred_element_type=f32)
                    for n in range(2):
                        j = at + n
                        pj, qj = p[:, n * tile : (n + 1) * tile], q[:, n * tile : (n + 1) * tile]
                        if last:
                            pj, qj = pj + vacc[1, j].astype(f32), qj + vacc[0, j].astype(f32)
                            near_j = jnp.where(u_near, qj, pj).astype(bf16)
                            cross_j = jnp.where(u_near, pj, qj).astype(bf16)
                            out_cross[j] = cross_j
                            if out_near is not None:
                                out_near[j] = near_j
                            if out_pair is not None:
                                out_pair[j] = near_j
                                out_pair[width + j] = cross_j
                        else:
                            vacc[0, j] = pj.astype(bf16)
                            vacc[1, j] = qj.astype(bf16)
                return 0

            lax.fori_loop(0, (cuts[k + 1] - cuts[k]) // 14, close, 0)
            if not last:
                carries[2 * k].start()
                carries[2 * k + 1].start()
            elif left:
                saves[k].start()
        for c in saves if last else carries:
            c.wait()


def terms(left, step, steps, info, table, envs, tensors, small, large, acc=None, onto=None):
    tile = envs[0].shape[-1]
    width = small.shape[0] // GROUP
    last = acc is not None
    final = step + 1 == steps
    pieces = len(envs) - 1
    env = pltpu.VMEM((width, tile, tile), bf16)
    total = jax.ShapeDtypeStruct((2, width, tile, tile), bf16)
    n = width * GROUP
    scratch = [
        pltpu.VMEM((tile, 3 * tile), bf16),
        pltpu.VMEM((tile, tile), bf16),
        pltpu.VMEM((tile, tile), bf16),
        pltpu.VMEM((tile, 3 * tile), bf16),
        *[pltpu.VMEM(shape, bf16) for _ in range(2) for shape in ((4, n, 2 * tile), (2, 2 * n, 2 * tile))],
        pltpu.VMEM((4, width, tile, tile), bf16),
        pltpu.VMEM((2, width, tile, tile), bf16),
        pltpu.VMEM((4, tile, tile), bf16),
        pltpu.VMEM((4, tile, tile), bf16),
        pltpu.VMEM((n, n), bf16),
        pltpu.VMEM((2 * n, 2 * n), bf16),
        pltpu.SemaphoreType.DMA((2, 3)),
        pltpu.SemaphoreType.DMA((4,)),
    ]
    if not last:
        scratch += [pltpu.VMEM((width, tile, tile), bf16)] * 2 + [pltpu.SemaphoreType.DMA((2, 3))]
    operands = [in_vmem(b) if last else b for b in envs] + [*tensors, in_hbm(small), in_hbm(large)]
    info_shape = jax.ShapeDtypeStruct(info.shape, info.dtype)
    out_specs, out_shape = [ANY, SMEM], [total, info_shape]
    aliases = {}
    if last:
        operands.append(acc)
        out_specs, out_shape = [VMEM, SMEM], [env, info_shape]
        if final or not left:
            out_specs.insert(0, VMEM)
            out_shape.insert(0, env)
        if not final:
            out_specs.insert(0, VMEM)
            out_shape.insert(0, pltpu.VMEM((2 * width, tile, tile), bf16))
        if left:
            if onto is not None:
                operands.append(onto)
                aliases = {1 + len(operands): 0}
            out_specs.insert(0, ANY)
            out_shape.insert(0, jax.ShapeDtypeStruct((steps, 1, width, tile, tile), bf16))
            scratch.append(pltpu.SemaphoreType.DMA((3,)))

    def body(info, table, *refs):
        refs = (refs[0], refs[1 : 1 + pieces]) + refs[1 + pieces :]
        terms_body(left, last, final, onto is not None, width, tile, step, steps, info, table, *refs)

    return pl.pallas_call(
        body,
        in_specs=[SMEM, SMEM] + [VMEM if last else ANY] * len(envs) + [ANY] * (len(operands) - len(envs)),
        out_specs=out_specs,
        out_shape=out_shape,
        scratch_shapes=scratch,
        input_output_aliases=aliases,
        compiler_params=pltpu.CompilerParams(vmem_limit_bytes=LIMIT),
    )(info, table, *operands)


def place_body(groups, count, direct, info, *refs):
    pieces = 3
    total = sum(len(sources) for _, _, sources in groups)
    sources, outs, held, sem = refs[:total], refs[-2 - count : -2], refs[-2], refs[-1]
    jobs = []
    for n, (out, index, flags) in enumerate(groups):
        dst = outs[out] if index is None else outs[out].at[index, 0]
        for flag in flags:
            src = sources[len(jobs)]
            cuts = [src.shape[0] * k // pieces for k in range(pieces + 1)]
            spans = [pl.ds(a, b - a) for a, b in zip(cuts, cuts[1:])]
            here = held.at[n]
            reads = [pltpu.make_async_copy(src.at[c], here.at[c], sem.at[0, n, k]) for k, c in enumerate(spans)]
            writes = [pltpu.make_async_copy(here.at[c], dst.at[c], sem.at[1, n, k]) for k, c in enumerate(spans)]
            if direct[len(jobs)]:
                reads, writes = [pltpu.make_async_copy(src.at[c], dst.at[c], sem.at[1, n, k]) for k, c in enumerate(spans)], None
            jobs.append((flag, reads, writes))

    for flag, reads, _ in jobs:

        @pl.when(flag(info))
        def _(reads=reads):
            for c in reads:
                c.start()

    for flag, reads, writes in jobs:

        @pl.when(flag(info))
        def _(reads=reads, writes=writes):
            for a, b in zip(reads, writes or ()):
                a.wait()
                b.start()

    for flag, reads, writes in jobs:

        @pl.when(flag(info))
        def _(reads=reads, writes=writes):
            for c in writes or reads:
                c.wait()


def place(info, groups, shapes, onto, resident=()):
    sources = [b for _, _, pairs in groups for _, b in pairs]
    specs = [VMEM if any(b is r for r in resident) else ANY for b in sources]
    sources = [in_vmem(b) if spec is VMEM else b for b, spec in zip(sources, specs)]
    plan = [(out, index, [flag for flag, _ in pairs]) for out, index, pairs in groups]
    return pl.pallas_call(
        functools.partial(place_body, plan, len(shapes), [spec is VMEM for spec in specs]),
        in_specs=[SMEM] + specs + [ANY] * len(onto),
        out_specs=[ANY] * len(shapes),
        out_shape=[jax.ShapeDtypeStruct(s, bf16) for s in shapes],
        scratch_shapes=[
            pltpu.VMEM((len(groups), *sources[0].shape), bf16),
            pltpu.SemaphoreType.DMA((2, len(groups), 3)),
        ],
        compiler_params=pltpu.CompilerParams(vmem_limit_bytes=LIMIT),
        input_output_aliases={1 + len(sources) + i: i for i in range(len(onto))},
    )(info, *sources, *onto)


def compact(mpo):
    sites, width = mpo.shape[:2]
    return jnp.transpose(mpo, (0, 3, 2, 4, 1)).reshape(sites, 4 * width, 4 * width)


def shards(site_tensors, mpo, left_in, right_in, tile_rows):
    chains, sectors = lax.axis_size("chain"), lax.axis_size("sector")
    routes = Routes(chains, sectors)
    chain, sector = lax.axis_index("chain"), lax.axis_index("sector")
    core, x = chain % 2, sector % 2
    sites, _, tile = site_tensors.shape[:3]
    same = core == x
    info = jnp.stack([(chain - core + x) * sites, sector // 2, x, same.astype(jnp.int32), chain]).astype(jnp.int32)

    left_near, right_own = left_in[0, 0], right_in[0, 0]
    width = left_near.shape[0]
    tensors = jnp.transpose(site_tensors[:, 0], (0, 2, 1, 3)).reshape(sites * 4, tile, tile)
    packed = jnp.concatenate([left_near, tensors])
    left_cross = move(packed, routes.left_cross)
    left_second, right_own, tensors, packed = lax.optimization_barrier((left_near, right_own, tensors, packed))
    left_near_below = move(left_second, routes.left_up)
    right_near_above = move(right_own, routes.right_native_down)
    right_near = move(right_own, routes.to_right_core)
    tensors_below = move(tensors, routes.left_up)
    tensors_right = move(tensors, routes.to_right_core)
    k = compact(mpo)
    k_right = move(k, routes.to_right_core)
    right_own, k_right = lax.optimization_barrier((right_own, k_right))
    cuts = [0, width // 2, width] if width % 2 == 0 else [0, width]
    right_cross = [move(right_own[a:b], routes.right_cross) for a, b in zip(cuts, cuts[1:])]
    ks = spread(info, k, k_right)
    left_cross, left_near_below, right_near_above, ks, tensors_below, tensors_right = lax.optimization_barrier(
        (left_cross, left_near_below, right_near_above, ks, tensors_below, tensors_right)
    )
    left_cross_below = move(left_cross, routes.left_up)
    tensors_cross_right = move(left_cross[width:], routes.to_right_core)
    right_cross_above = [move(b, routes.right_down) for b in right_cross]
    pair, pair_below = (tensors, left_cross), (tensors_below, left_cross_below)
    pair_right = (tensors_right, tensors_cross_right)

    l_far, r_far = (left_near_below, left_cross_below), (right_near_above, *right_cross_above)
    l, r = (in_hbm(left_near), left_cross), (right_near, *right_cross)

    def local(left, step, info, envs, tensors):
        return terms(left, step, sites, info, tile_rows, envs, tensors, ks[3 * step], ks[3 * step + 1])

    def remote(left, step, info, envs, tensors, acc, onto=None):
        return terms(left, step, sites, info, tile_rows, envs, tensors, ks[3 * step + 2], ks[3 * step + 1], acc, onto)

    envs_shape = (sites, 1, width, tile, tile)

    def own(info):
        return info[3] == 1

    def other(info):
        return info[3] != 1

    left_envs = right_envs = None
    kept = []
    info, tensors_cross_right = lax.optimization_barrier((info, tensors_cross_right))
    pair_right = (tensors_right, tensors_cross_right)
    l_acc, info = local(True, 0, info, l, pair)
    for step in range(sites):
        more = step + 1 < sites
        if step > 0:
            kept.append((step, left_back, list(right_back)))
        left_envs, l_first, l_cross, info = remote(True, step, info, l_far, pair_below, l_acc, left_envs)
        left_back = move(l_cross, routes.left_back)
        if more:
            l_far = [move(l_first, routes.left_up)]
        if step == 0:
            r_acc, info = local(False, step, info, r, pair_right)
        if step > 0:
            info, *kept[-1][2][:] = lax.optimization_barrier((info, *kept[-1][2]))
        *r_pair, r_near, r_cross, info = remote(False, step, info, r_far, pair_right, r_acc)
        if more:
            l_acc, info = local(True, step + 1, info, [l_first], pair)
        if more:
            r_far = [move(r_pair[0], routes.right_down)]
            info, left_back = lax.optimization_barrier((info, left_back))
        right_back = (move(r_near, routes.from_right_core), move(r_cross, routes.right_back))
        if more:
            r_acc, info = local(False, step + 1, info, r_pair, pair_right)
    info, left_back = lax.optimization_barrier((info, left_back))
    for step, back, backs in kept:
        left_envs, right_envs = place(
            info,
            [(0, step - 1, [(other, back)]), (1, sites - step, list(zip((own, other), backs)))],
            [envs_shape] * 2,
            [left_envs] + ([] if right_envs is None else [right_envs]),
        )

    edge_tile = move(jnp.where(same, l_first, left_back), routes.edge_same + routes.edge_other)
    edge = [
        (lambda info: info[4] == 0, left_in[0, 0]),
        (lambda info: info[4] != 0, edge_tile),
    ]
    left_envs, right_envs, left_edge = place(
        info,
        [(0, sites - 1, [(other, left_back)]), (1, 0, list(zip((own, other), right_back))), (2, None, edge)],
        [envs_shape, envs_shape, (width, tile, tile)],
        [left_envs] + ([] if right_envs is None else [right_envs]),
        [left_back, *right_back, edge_tile],
    )
    return left_envs, right_envs, left_edge[None, None]


def solution(mesh):
    placed = (
        P("chain", "sector", None, None, None),
        P("chain", None, None, None, None),
        P("chain", "sector", None, None, None),
        P("chain", "sector", None, None, None),
        P(),
    )
    return jax.shard_map(
        shards,
        mesh=mesh,
        in_specs=placed,
        out_specs=(
            P("chain", "sector", None, None, None),
            P("chain", "sector", None, None, None),
            P("chain", "sector", None, None, None),
        ),
        check_vma=False,
    )
```

```python
import functools

import jax
import jax.numpy as jnp
from jax import lax
from jax.experimental import pallas as pl
from jax.experimental.pallas import tpu as pltpu
from jax.sharding import PartitionSpec as P

f32 = jnp.float32
bf16 = jnp.bfloat16
AXES = ("chain", "sector")
SUBLANES = 8
GROUP = SUBLANES // 2
STEP_ROWS = 2 * SUBLANES
ROWS_16_BIT = 16
ANY = pl.BlockSpec(memory_space=pl.ANY)
SMEM = pl.BlockSpec(memory_space=pltpu.SMEM)
VMEM = pl.BlockSpec(memory_space=pltpu.VMEM)
LIMIT = 18 * 2**20


class Routes:
    def __init__(self, chains, sectors):
        def at(pair, core, z, x):
            return (2 * pair + core) * sectors + 2 * z + x

        pairs, zs = range(chains // 2), range(sectors // 2)
        every = [(y, z, e) for y in pairs for z in zs for e in (0, 1)]
        below = [(y, z, e) for y, z, e in every if z + 1 in zs]
        self.left_cross = [(at(y, e, z, 1 - e), at(y, e, z, e)) for y, z, e in every]
        self.right_cross = [(at(y, e, z, 1 - e), at(y, 1 - e, z, e)) for y, z, e in every]
        self.to_right_core = [(at(y, e, z, e), at(y, 1 - e, z, e)) for y, z, e in every]
        self.left_up = [(at(y, e, z, e), at(y, e, z + 1, e)) for y, z, e in below]
        self.right_down = [(at(y, 1 - e, z + 1, e), at(y, 1 - e, z, e)) for y, z, e in below]
        self.right_native_down = [(at(y, e, z + 1, e), at(y, 1 - e, z, e)) for y, z, e in below]
        self.left_back = [(b, a) for a, b in self.left_cross]
        self.right_back = [(b, a) for a, b in self.right_cross]
        self.from_right_core = [(b, a) for a, b in self.to_right_core]
        shifts = [(c, q) for c in range(chains - 1) for q in range(sectors)]
        self.edge_same = [(c * sectors + q, (c + 1) * sectors + q) for c, q in shifts if c % 2 == q % 2]
        self.edge_other = [(c * sectors + q, (c + 1) * sectors + q) for c, q in shifts if c % 2 != q % 2]


def move(block, route):
    return lax.ppermute(block, AXES, route)


def in_hbm(x):
    return pltpu.with_memory_space_constraint(x, pltpu.HBM)


def in_vmem(x):
    return pltpu.with_memory_space_constraint(x, pltpu.VMEM)


def spread_body(width, steps, info, own, received, *outs):
    def spread(k, states, flip):
        n = len(states) * width * GROUP
        cols = 4 * width
        row = lax.broadcasted_iota(jnp.int32, (n, cols), 0) // GROUP
        col = lax.broadcasted_iota(jnp.int32, (n, cols), 1)
        pick = jnp.where(row + states[0] * width == col, 1.0, 0.0)
        if not flip:
            mid = jnp.dot(pick.astype(bf16), k, preferred_element_type=f32).astype(bf16)
            out = lax.dot_general(
                mid, pick.astype(bf16), (((1,), (1,)), ((), ())), preferred_element_type=f32
            )
        else:
            out = jnp.zeros((n, n), f32)
            group = lax.broadcasted_iota(jnp.int32, (n, width), 0) // GROUP
            inner = lax.broadcasted_iota(jnp.int32, (n, width), 1)
            tall = [jnp.where(group - i * width == inner, 1.0, 0.0).astype(bf16) for i in range(len(states))]
            for i, a in enumerate(states):
                for j, b in enumerate(states):
                    block = k[a * width : (a + 1) * width, b * width : (b + 1) * width]
                    mid = lax.dot_general(
                        tall[i], block, (((1,), (1,)), ((), ())), preferred_element_type=f32
                    ).astype(bf16)
                    out += lax.dot_general(
                        mid, tall[j], (((1,), (1,)), ((), ())), preferred_element_type=f32
                    )
        i = lax.broadcasted_iota(jnp.int32, out.shape, 0) % GROUP
        j = lax.broadcasted_iota(jnp.int32, out.shape, 1) % GROUP
        out = jnp.where(i == j, out, 0.0)
        more = -out.shape[0] % ROWS_16_BIT
        if more:
            out = jnp.concatenate([out, jnp.zeros((more, out.shape[1]), f32)], axis=0)
        return out.astype(bf16)

    def fill(source, flip):
        for step in range(steps):
            k = source[steps - 1 - step if flip else step]
            for i, states in enumerate(((0,), (1, 2), (3,))):
                outs[3 * step + i][...] = spread(k, states, flip)

    @pl.when(info[3] == 1)
    def _():
        fill(own, False)

    @pl.when(info[3] != 1)
    def _():
        fill(received, True)


def spread(info, own, received):
    steps, width = own.shape[0], own.shape[1] // 4
    n = width * GROUP
    shapes = [(n + -n % ROWS_16_BIT, n), (2 * n + -2 * n % ROWS_16_BIT, 2 * n), (n + -n % ROWS_16_BIT, n)] * steps
    return pl.pallas_call(
        functools.partial(spread_body, width, steps),
        in_specs=[SMEM, VMEM, VMEM],
        out_specs=[VMEM] * len(shapes),
        out_shape=[pltpu.HBM(s, bf16) for s in shapes],
        compiler_params=pltpu.CompilerParams(vmem_limit_bytes=LIMIT),
    )(info, own, received)


def terms_body(left, last, final, onto, width, tile, step, steps, info, table, pair, pieces, a_near, a_cross, small, large, *rest):
    joined = not pieces
    if last:
        acc, *rest = rest
        if left:
            rest = rest[1:] if onto else rest
            envs, *rest = rest
            *rest, envs_sem = rest
        out_pair = out_near = None
        if not final:
            out_pair, *rest = rest
        if final or not left:
            out_near, *rest = rest
        out_cross, info_out, *rest = rest
    else:
        acc, info_out, *rest = rest
    bd, bm, cp, cq, one0, two0, one1, two1, z, vacc, an, ac, ks, kd, sem, weight_sem, *rest = rest
    first, zpos, x, same = info[0], info[1], info[2], info[3]
    for i in range(info.shape[0]):
        info_out[i] = info[i]
    active = same if left else 1 - same
    u_near = (x == 0) if left else (x == 1)
    cuts = [0, width // 6 * 2, width // 6 * 4, width]
    site = step if left else steps - 1 - step

    def carry(which, k):
        c = pl.ds(cuts[k], cuts[k + 1] - cuts[k])
        ends = (acc.at[which, c], vacc.at[which, c])
        return pltpu.make_async_copy(*(ends if last else ends[::-1]), sem.at[which, k])

    def save(k):
        c = pl.ds(cuts[k], cuts[k + 1] - cuts[k])
        return pltpu.make_async_copy((out_pair if out_near is None else out_near).at[c], envs.at[step, 0, c], envs_sem.at[k])

    carries = [carry(which, k) for k in range(3) for which in range(2)]
    saves = [save(k) for k in range(3)] if last and left else []
    factors = [
        pltpu.make_async_copy(src.at[pl.ds(src.shape[0] - 4 * (steps - site), 4)], dst, weight_sem.at[i])
        for i, (src, dst) in enumerate(((a_near, an), (a_cross, ac)))
    ]
    weights = [
        pltpu.make_async_copy(src, dst, weight_sem.at[2 + i]) for i, (src, dst) in enumerate(((small, ks), (large, kd)))
    ]
    fetches = []
    share = width // max(len(pieces), 1)
    if rest:
        near, cross, fetch_sem = rest
        for k in range(3):
            c = pl.ds(cuts[k], cuts[k + 1] - cuts[k])
            fetches.append(pltpu.make_async_copy(pair.at[c], near.at[c], fetch_sem.at[0, k]))
            if joined or len(pieces) == 1:
                src = pair.at[pl.ds(width + cuts[k], cuts[k + 1] - cuts[k])] if joined else pieces[0].at[c]
                fetches.append(pltpu.make_async_copy(src, cross.at[c], fetch_sem.at[1, k]))
        if len(pieces) > 1:
            for k, src in enumerate(pieces):
                dst = cross.at[pl.ds(k * share, share)]
                fetches.append(pltpu.make_async_copy(src, dst, fetch_sem.at[1, k]))
        crosses = [cross]
    elif joined:
        near, crosses = pair.at[pl.ds(0, width)], [pair.at[pl.ds(width, width)]]
    else:
        near, crosses = pair, [piece.at[pl.ds(0, share)] for piece in pieces]

    @pl.when(active == 1)
    def _():
        for c in factors + fetches + weights + (carries if last else []):
            c.start()
        count = table.shape[1]
        source_bond = first + (site if left else site + 1)
        target_bond = first + (site + 1 if left else site)
        sign = 1 if left else -1
        u = 2 * zpos if left else 2 * zpos + 1
        v = u + sign
        far_u, far_v = u - 2 * sign, v - 2 * sign

        def rows_of(bond, index):
            safe = jnp.clip(index, 0, count - 1)
            return jnp.where((index >= 0) & (index < count), table[bond, safe], 0)

        sub = lax.broadcasted_iota(jnp.int32, (tile, tile), 0)
        lane = lax.broadcasted_iota(jnp.int32, (tile, tile), 1)

        def factor(of_u, state, source, target):
            a = jnp.where(u_near if of_u else jnp.logical_not(u_near), an[state].astype(f32), ac[state].astype(f32))
            a = a if left else a.T
            keep = (sub < rows_of(source_bond, source)) & (lane < rows_of(target_bond, target))
            return jnp.where(keep, a, 0.0)

        for c in factors:
            c.wait()
        if last:
            dual = [factor(False, 3, far_v, v)] + [factor(not left, t, far_v, u) for t in (1, 2)]
            mono = factor(True, 3, far_u, u)
        else:
            dual = [factor(True, 0, u, u)] + [factor(left, t, u, v) for t in (1, 2)]
            mono = factor(False, 0, v, v)
        for i, m in enumerate(dual):
            bd[:, i * tile : (i + 1) * tile] = m.astype(bf16)
        bm[...] = mono.astype(bf16)
        cp[...] = dual[0].T.astype(bf16)
        for i, m in enumerate((dual[1], dual[2], mono)):
            cq[:, i * tile : (i + 1) * tile] = m.T.astype(bf16)

        dual_near = jnp.logical_not(u_near) if last else u_near

        for f in fetches:
            f.wait()
        n = width * GROUP

        def exchange(a, b):
            upper = lax.broadcasted_iota(jnp.int32, a.shape, 1) < GROUP
            return (
                jnp.where(upper, a, pltpu.roll(b, GROUP, 1)),
                jnp.where(upper, pltpu.roll(a, GROUP, 1), b),
            )

        def split(part):
            pairs = part.reshape(width // 2, 2, SUBLANES, tile)
            return jnp.concatenate([h.reshape(n, tile) for h in exchange(pairs[:, 0], pairs[:, 1])], axis=1)

        def joined_rows(part):
            part = part.reshape(width // 2, SUBLANES, 2 * tile)
            a, b = exchange(part[..., :tile], part[..., tile:])
            return jnp.stack([a, b], axis=1).reshape(width, SUBLANES, tile)

        def products(i, slots):
            one, two = slots
            r = pl.ds(pl.multiple_of(i * STEP_ROWS, STEP_ROWS), STEP_ROWS)
            e_n = near[:, r, :]
            e_c = jnp.concatenate([c[:, r, :] for c in crosses], axis=0)
            e_d = jnp.where(dual_near, e_n, e_c).reshape(width * STEP_ROWS, tile)
            e_m = jnp.where(dual_near, e_c, e_n).reshape(width * STEP_ROWS, tile)
            yd = jnp.dot(e_d, bd[...], preferred_element_type=f32).reshape(width, STEP_ROWS, 3 * tile)
            ym = jnp.dot(e_m, bm[...], preferred_element_type=f32).reshape(width, STEP_ROWS, tile)
            for h in range(2):
                c = slice(h * SUBLANES, (h + 1) * SUBLANES)
                one[2 * h] = split(yd[:, c, :tile]).astype(bf16)
                one[2 * h + 1] = split(ym[:, c, :]).astype(bf16)
                two[h] = jnp.concatenate(
                    [split(yd[:, c, t * tile : (t + 1) * tile]) for t in (1, 2)], axis=0
                ).astype(bf16)

        def mix(i, slots):
            one, two = slots
            r = pl.ds(pl.multiple_of(i * STEP_ROWS, STEP_ROWS), STEP_ROWS)

            def put(to, halves):
                z[to, :, r, :] = jnp.concatenate([joined_rows(x) for x in halves], axis=1).astype(bf16)

            for m, to in ((0, 0), (1, 3)):
                put(to, [jnp.dot(ks[...], one[2 * h + m], preferred_element_type=f32)[:n] for h in range(2)])
            mixed = [jnp.dot(kd[...], two[h], preferred_element_type=f32) for h in range(2)]
            for t in range(2):
                put(1 + t, [x[t * n : (t + 1) * n] for x in mixed])

        y0, y1 = (one0, two0), (one1, two1)
        count_rows = tile // STEP_ROWS
        products(0, y0)
        for c in weights:
            c.wait()

        def turn(j, _):
            for k in range(2 // 2):
                i = 2 * j + 2 * k
                products(i + 1, y1)
                mix(i, y0)
                products(jnp.minimum(i + 2, count_rows - 2), y0)
                mix(i + 1, y1)
            return 0

        lax.fori_loop(0, count_rows // 2, turn, 0)
        if last:
            for c in carries:
                c.wait()
        for k in range(3):
            def close(m, _, k=k):
                for i in range(7):
                    at = cuts[k] + 2 * (m * 7 + i)
                    p = jnp.dot(cp[...], jnp.concatenate([z[0, at], z[0, at + 1]], axis=1), preferred_element_type=f32)
                    zq = [z[1:4, at + n].reshape(3 * tile, tile) for n in range(2)]
                    q = jnp.dot(cq[...], jnp.concatenate(zq, axis=1), preferred_element_type=f32)
                    for n in range(2):
                        j = at + n
                        pj, qj = p[:, n * tile : (n + 1) * tile], q[:, n * tile : (n + 1) * tile]
                        if last:
                            pj, qj = pj + vacc[1, j].astype(f32), qj + vacc[0, j].astype(f32)
                            near_j = jnp.where(u_near, qj, pj).astype(bf16)
                            cross_j = jnp.where(u_near, pj, qj).astype(bf16)
                            out_cross[j] = cross_j
                            if out_near is not None:
                                out_near[j] = near_j
                            if out_pair is not None:
                                out_pair[j] = near_j
                                out_pair[width + j] = cross_j
                        else:
                            vacc[0, j] = pj.astype(bf16)
                            vacc[1, j] = qj.astype(bf16)
                return 0

            lax.fori_loop(0, (cuts[k + 1] - cuts[k]) // 14, close, 0)
            if not last:
                carries[2 * k].start()
                carries[2 * k + 1].start()
            elif left:
                saves[k].start()
        for c in saves if last else carries:
            c.wait()


def terms(left, step, steps, info, table, envs, tensors, small, large, acc=None, onto=None):
    tile = envs[0].shape[-1]
    width = small.shape[1] // GROUP
    last = acc is not None
    final = step + 1 == steps
    pieces = len(envs) - 1
    env = pltpu.VMEM((width, tile, tile), bf16)
    total = jax.ShapeDtypeStruct((2, width, tile, tile), bf16)
    n = width * GROUP
    scratch = [
        pltpu.VMEM((tile, 3 * tile), bf16),
        pltpu.VMEM((tile, tile), bf16),
        pltpu.VMEM((tile, tile), bf16),
        pltpu.VMEM((tile, 3 * tile), bf16),
        *[pltpu.VMEM(shape, bf16) for _ in range(2) for shape in ((4, n, 2 * tile), (2, 2 * n, 2 * tile))],
        pltpu.VMEM((4, width, tile, tile), bf16),
        pltpu.VMEM((2, width, tile, tile), bf16),
        pltpu.VMEM((4, tile, tile), bf16),
        pltpu.VMEM((4, tile, tile), bf16),
        pltpu.VMEM(small.shape, bf16),
        pltpu.VMEM(large.shape, bf16),
        pltpu.SemaphoreType.DMA((2, 3)),
        pltpu.SemaphoreType.DMA((4,)),
    ]
    if not last:
        scratch += [pltpu.VMEM((width, tile, tile), bf16)] * 2 + [pltpu.SemaphoreType.DMA((2, 3))]
    operands = [in_vmem(b) if last else b for b in envs] + [*tensors, in_hbm(small), in_hbm(large)]
    info_shape = jax.ShapeDtypeStruct(info.shape, info.dtype)
    out_specs, out_shape = [ANY, SMEM], [total, info_shape]
    aliases = {}
    if last:
        operands.append(acc)
        out_specs, out_shape = [VMEM, SMEM], [env, info_shape]
        if final or not left:
            out_specs.insert(0, VMEM)
            out_shape.insert(0, env)
        if not final:
            out_specs.insert(0, VMEM)
            out_shape.insert(0, pltpu.VMEM((2 * width, tile, tile), bf16))
        if left:
            if onto is not None:
                operands.append(onto)
                aliases = {1 + len(operands): 0}
            out_specs.insert(0, ANY)
            out_shape.insert(0, jax.ShapeDtypeStruct((steps, 1, width, tile, tile), bf16))
            scratch.append(pltpu.SemaphoreType.DMA((3,)))

    def body(info, table, *refs):
        refs = (refs[0], refs[1 : 1 + pieces]) + refs[1 + pieces :]
        terms_body(left, last, final, onto is not None, width, tile, step, steps, info, table, *refs)

    return pl.pallas_call(
        body,
        in_specs=[SMEM, SMEM] + [VMEM if last else ANY] * len(envs) + [ANY] * (len(operands) - len(envs)),
        out_specs=out_specs,
        out_shape=out_shape,
        scratch_shapes=scratch,
        input_output_aliases=aliases,
        compiler_params=pltpu.CompilerParams(vmem_limit_bytes=LIMIT),
    )(info, table, *operands)


def place_body(groups, count, direct, info, *refs):
    pieces = 3
    total = sum(len(sources) for _, _, sources in groups)
    sources, outs, held, sem = refs[:total], refs[-2 - count : -2], refs[-2], refs[-1]
    jobs = []
    for n, (out, index, flags) in enumerate(groups):
        dst = outs[out] if index is None else outs[out].at[index, 0]
        for flag in flags:
            src = sources[len(jobs)]
            cuts = [src.shape[0] * k // pieces for k in range(pieces + 1)]
            spans = [pl.ds(a, b - a) for a, b in zip(cuts, cuts[1:])]
            here = held.at[n]
            reads = [pltpu.make_async_copy(src.at[c], here.at[c], sem.at[0, n, k]) for k, c in enumerate(spans)]
            writes = [pltpu.make_async_copy(here.at[c], dst.at[c], sem.at[1, n, k]) for k, c in enumerate(spans)]
            if direct[len(jobs)]:
                reads, writes = [pltpu.make_async_copy(src.at[c], dst.at[c], sem.at[1, n, k]) for k, c in enumerate(spans)], None
            jobs.append((flag, reads, writes))

    for flag, reads, _ in jobs:

        @pl.when(flag(info))
        def _(reads=reads):
            for c in reads:
                c.start()

    for flag, reads, writes in jobs:

        @pl.when(flag(info))
        def _(reads=reads, writes=writes):
            for a, b in zip(reads, writes or ()):
                a.wait()
                b.start()

    for flag, reads, writes in jobs:

        @pl.when(flag(info))
        def _(reads=reads, writes=writes):
            for c in writes or reads:
                c.wait()


def place(info, groups, shapes, onto, resident=()):
    sources = [b for _, _, pairs in groups for _, b in pairs]
    specs = [VMEM if any(b is r for r in resident) else ANY for b in sources]
    sources = [in_vmem(b) if spec is VMEM else b for b, spec in zip(sources, specs)]
    plan = [(out, index, [flag for flag, _ in pairs]) for out, index, pairs in groups]
    return pl.pallas_call(
        functools.partial(place_body, plan, len(shapes), [spec is VMEM for spec in specs]),
        in_specs=[SMEM] + specs + [ANY] * len(onto),
        out_specs=[ANY] * len(shapes),
        out_shape=[jax.ShapeDtypeStruct(s, bf16) for s in shapes],
        scratch_shapes=[
            pltpu.VMEM((len(groups), *sources[0].shape), bf16),
            pltpu.SemaphoreType.DMA((2, len(groups), 3)),
        ],
        compiler_params=pltpu.CompilerParams(vmem_limit_bytes=LIMIT),
        input_output_aliases={1 + len(sources) + i: i for i in range(len(onto))},
    )(info, *sources, *onto)


def compact(mpo):
    sites, width = mpo.shape[:2]
    return jnp.transpose(mpo, (0, 3, 2, 4, 1)).reshape(sites, 4 * width, 4 * width)


def shards(site_tensors, mpo, left_in, right_in, tile_rows):
    chains, sectors = lax.axis_size("chain"), lax.axis_size("sector")
    routes = Routes(chains, sectors)
    chain, sector = lax.axis_index("chain"), lax.axis_index("sector")
    core, x = chain % 2, sector % 2
    sites, _, tile = site_tensors.shape[:3]
    same = core == x
    info = jnp.stack([(chain - core + x) * sites, sector // 2, x, same.astype(jnp.int32), chain]).astype(jnp.int32)

    left_near, right_own = left_in[0, 0], right_in[0, 0]
    width = left_near.shape[0]
    tensors = jnp.transpose(site_tensors[:, 0], (0, 2, 1, 3)).reshape(sites * 4, tile, tile)
    packed = jnp.concatenate([left_near, tensors])
    left_cross = move(packed, routes.left_cross)
    left_second, right_own, tensors, packed = lax.optimization_barrier((left_near, right_own, tensors, packed))
    left_near_below = move(left_second, routes.left_up)
    right_near_above = move(right_own, routes.right_native_down)
    right_near = move(right_own, routes.to_right_core)
    tensors_below = move(tensors, routes.left_up)
    tensors_right = move(tensors, routes.to_right_core)
    k = compact(mpo)
    k_right = move(k, routes.to_right_core)
    right_own, k_right = lax.optimization_barrier((right_own, k_right))
    cuts = [0, width // 2, width] if width % 2 == 0 else [0, width]
    right_cross = [move(right_own[a:b], routes.right_cross) for a, b in zip(cuts, cuts[1:])]
    ks = spread(info, k, k_right)
    left_cross, left_near_below, right_near_above, ks, tensors_below, tensors_right = lax.optimization_barrier(
        (left_cross, left_near_below, right_near_above, ks, tensors_below, tensors_right)
    )
    left_cross_below = move(left_cross, routes.left_up)
    tensors_cross_right = move(left_cross[width:], routes.to_right_core)
    right_cross_above = [move(b, routes.right_down) for b in right_cross]
    pair, pair_below = (tensors, left_cross), (tensors_below, left_cross_below)
    pair_right = (tensors_right, tensors_cross_right)

    l_far, r_far = (left_near_below, left_cross_below), (right_near_above, *right_cross_above)
    l, r = (in_hbm(left_near), left_cross), (right_near, *right_cross)

    def local(left, step, info, envs, tensors):
        return terms(left, step, sites, info, tile_rows, envs, tensors, ks[3 * step], ks[3 * step + 1])

    def remote(left, step, info, envs, tensors, acc, onto=None):
        return terms(left, step, sites, info, tile_rows, envs, tensors, ks[3 * step + 2], ks[3 * step + 1], acc, onto)

    envs_shape = (sites, 1, width, tile, tile)

    def own(info):
        return info[3] == 1

    def other(info):
        return info[3] != 1

    left_envs = right_envs = None
    kept = []
    info, tensors_cross_right = lax.optimization_barrier((info, tensors_cross_right))
    pair_right = (tensors_right, tensors_cross_right)
    l_acc, info = local(True, 0, info, l, pair)
    for step in range(sites):
        more = step + 1 < sites
        if step > 0:
            kept.append((step, left_back, list(right_back)))
        left_envs, l_first, l_cross, info = remote(True, step, info, l_far, pair_below, l_acc, left_envs)
        left_back = move(l_cross, routes.left_back)
        if more:
            l_far = [move(l_first, routes.left_up)]
        if step == 0:
            r_acc, info = local(False, step, info, r, pair_right)
        if step > 0:
            info, *kept[-1][2][:] = lax.optimization_barrier((info, *kept[-1][2]))
        *r_pair, r_near, r_cross, info = remote(False, step, info, r_far, pair_right, r_acc)
        if more:
            l_acc, info = local(True, step + 1, info, [l_first], pair)
        if more:
            r_far = [move(r_pair[0], routes.right_down)]
            info, left_back = lax.optimization_barrier((info, left_back))
        right_back = (move(r_near, routes.from_right_core), move(r_cross, routes.right_back))
        if more:
            r_acc, info = local(False, step + 1, info, r_pair, pair_right)
    info, left_back = lax.optimization_barrier((info, left_back))
    for step, back, backs in kept:
        left_envs, right_envs = place(
            info,
            [(0, step - 1, [(other, back)]), (1, sites - step, list(zip((own, other), backs)))],
            [envs_shape] * 2,
            [left_envs] + ([] if right_envs is None else [right_envs]),
        )

    edge_tile = move(jnp.where(same, l_first, left_back), routes.edge_same + routes.edge_other)
    edge = [
        (lambda info: info[4] == 0, left_in[0, 0]),
        (lambda info: info[4] != 0, edge_tile),
    ]
    left_envs, right_envs, left_edge = place(
        info,
        [(0, sites - 1, [(other, left_back)]), (1, 0, list(zip((own, other), right_back))), (2, None, edge)],
        [envs_shape, envs_shape, (width, tile, tile)],
        [left_envs] + ([] if right_envs is None else [right_envs]),
        [left_back, *right_back, edge_tile],
    )
    return left_envs, right_envs, left_edge[None, None]


def solution(mesh):
    placed = (
        P("chain", "sector", None, None, None),
        P("chain", None, None, None, None),
        P("chain", "sector", None, None, None),
        P("chain", "sector", None, None, None),
        P(),
    )
    return jax.shard_map(
        shards,
        mesh=mesh,
        in_specs=placed,
        out_specs=(
            P("chain", "sector", None, None, None),
            P("chain", "sector", None, None, None),
            P("chain", "sector", None, None, None),
        ),
        check_vma=False,
    )
```

```python
import functools

import jax
import jax.numpy as jnp
from jax import lax
from jax.experimental import pallas as pl
from jax.experimental.pallas import tpu as pltpu
from jax.sharding import PartitionSpec as P

f32 = jnp.float32
bf16 = jnp.bfloat16
AXES = ("chain", "sector")
SUBLANES = 8
GROUP = SUBLANES // 2
STEP_ROWS = 2 * SUBLANES
ROWS_16_BIT = 16
ANY = pl.BlockSpec(memory_space=pl.ANY)
SMEM = pl.BlockSpec(memory_space=pltpu.SMEM)
VMEM = pl.BlockSpec(memory_space=pltpu.VMEM)
LIMIT = 18 * 2**20


class Routes:
    def __init__(self, chains, sectors):
        def at(pair, core, z, x):
            return (2 * pair + core) * sectors + 2 * z + x

        pairs, zs = range(chains // 2), range(sectors // 2)
        every = [(y, z, e) for y in pairs for z in zs for e in (0, 1)]
        below = [(y, z, e) for y, z, e in every if z + 1 in zs]
        self.left_cross = [(at(y, e, z, 1 - e), at(y, e, z, e)) for y, z, e in every]
        self.right_cross = [(at(y, e, z, 1 - e), at(y, 1 - e, z, e)) for y, z, e in every]
        self.to_right_core = [(at(y, e, z, e), at(y, 1 - e, z, e)) for y, z, e in every]
        self.left_up = [(at(y, e, z, e), at(y, e, z + 1, e)) for y, z, e in below]
        self.right_down = [(at(y, 1 - e, z + 1, e), at(y, 1 - e, z, e)) for y, z, e in below]
        self.right_native_down = [(at(y, e, z + 1, e), at(y, 1 - e, z, e)) for y, z, e in below]
        self.left_back = [(b, a) for a, b in self.left_cross]
        self.right_back = [(b, a) for a, b in self.right_cross]
        self.from_right_core = [(b, a) for a, b in self.to_right_core]
        shifts = [(c, q) for c in range(chains - 1) for q in range(sectors)]
        self.edge_same = [(c * sectors + q, (c + 1) * sectors + q) for c, q in shifts if c % 2 == q % 2]
        self.edge_other = [(c * sectors + q, (c + 1) * sectors + q) for c, q in shifts if c % 2 != q % 2]


def move(block, route):
    return lax.ppermute(block, AXES, route)


def in_hbm(x):
    return pltpu.with_memory_space_constraint(x, pltpu.HBM)


def in_vmem(x):
    return pltpu.with_memory_space_constraint(x, pltpu.VMEM)


def spread_body(width, steps, info, own, received, *outs):
    def spread(k, states, flip):
        n = len(states) * width * GROUP
        cols = 4 * width
        row = lax.broadcasted_iota(jnp.int32, (n, cols), 0) // GROUP
        col = lax.broadcasted_iota(jnp.int32, (n, cols), 1)
        pick = jnp.where(row + states[0] * width == col, 1.0, 0.0)
        if not flip:
            mid = jnp.dot(pick.astype(bf16), k, preferred_element_type=f32).astype(bf16)
            out = lax.dot_general(
                mid, pick.astype(bf16), (((1,), (1,)), ((), ())), preferred_element_type=f32
            )
        else:
            out = jnp.zeros((n, n), f32)
            group = lax.broadcasted_iota(jnp.int32, (n, width), 0) // GROUP
            inner = lax.broadcasted_iota(jnp.int32, (n, width), 1)
            tall = [jnp.where(group - i * width == inner, 1.0, 0.0).astype(bf16) for i in range(len(states))]
            for i, a in enumerate(states):
                for j, b in enumerate(states):
                    block = k[a * width : (a + 1) * width, b * width : (b + 1) * width]
                    mid = lax.dot_general(
                        tall[i], block, (((1,), (1,)), ((), ())), preferred_element_type=f32
                    ).astype(bf16)
                    out += lax.dot_general(
                        mid, tall[j], (((1,), (1,)), ((), ())), preferred_element_type=f32
                    )
        i = lax.broadcasted_iota(jnp.int32, out.shape, 0) % GROUP
        j = lax.broadcasted_iota(jnp.int32, out.shape, 1) % GROUP
        out = jnp.where(i == j, out, 0.0)
        more = -out.shape[0] % ROWS_16_BIT
        if more:
            out = jnp.concatenate([out, jnp.zeros((more, out.shape[1]), f32)], axis=0)
        return out.astype(bf16)

    def fill(source, flip):
        for step in range(steps):
            k = source[steps - 1 - step if flip else step]
            for i, states in enumerate(((0,), (1, 2), (3,))):
                outs[3 * step + i][...] = spread(k, states, flip)

    @pl.when(info[3] == 1)
    def _():
        fill(own, False)

    @pl.when(info[3] != 1)
    def _():
        fill(received, True)


def spread(info, own, received):
    steps, width = own.shape[0], own.shape[1] // 4
    n = width * GROUP
    shapes = [(n + -n % ROWS_16_BIT, n), (2 * n + -2 * n % ROWS_16_BIT, 2 * n), (n + -n % ROWS_16_BIT, n)] * steps
    return pl.pallas_call(
        functools.partial(spread_body, width, steps),
        in_specs=[SMEM, VMEM, VMEM],
        out_specs=[VMEM] * len(shapes),
        out_shape=[pltpu.HBM(s, bf16) for s in shapes],
        compiler_params=pltpu.CompilerParams(vmem_limit_bytes=LIMIT),
    )(info, own, received)


def terms_body(left, last, final, onto, width, tile, step, steps, info, table, pair, pieces, a_near, a_cross, small, large, *rest):
    joined = not pieces
    if last:
        acc, *rest = rest
        if left:
            rest = rest[1:] if onto else rest
            envs, *rest = rest
            *rest, envs_sem = rest
        out_pair = out_near = None
        if not final:
            out_pair, *rest = rest
        if final or not left:
            out_near, *rest = rest
        out_cross, info_out, *rest = rest
    else:
        acc, info_out, *rest = rest
    bd, bm, cp, cq, one0, two0, one1, two1, z, vacc, an, ac, ks, kd, sem, weight_sem, *rest = rest
    first, zpos, x, same = info[0], info[1], info[2], info[3]
    for i in range(info.shape[0]):
        info_out[i] = info[i]
    active = same if left else 1 - same
    u_near = (x == 0) if left else (x == 1)
    cuts = [0, width // 6 * 2, width // 6 * 4, width]
    site = step if left else steps - 1 - step

    def carry(which, k):
        c = pl.ds(cuts[k], cuts[k + 1] - cuts[k])
        ends = (acc.at[which, c], vacc.at[which, c])
        return pltpu.make_async_copy(*(ends if last else ends[::-1]), sem.at[which, k])

    def save(k):
        c = pl.ds(cuts[k], cuts[k + 1] - cuts[k])
        return pltpu.make_async_copy((out_pair if out_near is None else out_near).at[c], envs.at[step, 0, c], envs_sem.at[k])

    carries = [carry(which, k) for k in range(3) for which in range(2)]
    saves = [save(k) for k in range(3)] if last and left else []
    factors = [
        pltpu.make_async_copy(src.at[pl.ds(src.shape[0] - 4 * (steps - site), 4)], dst, weight_sem.at[i])
        for i, (src, dst) in enumerate(((a_near, an), (a_cross, ac)))
    ]
    weights = [
        pltpu.make_async_copy(src, dst, weight_sem.at[2 + i]) for i, (src, dst) in enumerate(((small, ks), (large, kd)))
    ]
    fetches = []
    share = width // max(len(pieces), 1)
    if rest:
        near, cross, fetch_sem = rest
        for k in range(3):
            c = pl.ds(cuts[k], cuts[k + 1] - cuts[k])
            fetches.append(pltpu.make_async_copy(pair.at[c], near.at[c], fetch_sem.at[0, k]))
            if joined or len(pieces) == 1:
                src = pair.at[pl.ds(width + cuts[k], cuts[k + 1] - cuts[k])] if joined else pieces[0].at[c]
                fetches.append(pltpu.make_async_copy(src, cross.at[c], fetch_sem.at[1, k]))
        if len(pieces) > 1:
            for k, src in enumerate(pieces):
                dst = cross.at[pl.ds(k * share, share)]
                fetches.append(pltpu.make_async_copy(src, dst, fetch_sem.at[1, k]))
        crosses = [cross]
    elif joined:
        near, crosses = pair.at[pl.ds(0, width)], [pair.at[pl.ds(width, width)]]
    else:
        near, crosses = pair, [piece.at[pl.ds(0, share)] for piece in pieces]

    @pl.when(active == 1)
    def _():
        for c in factors + fetches + weights + (carries if last else []):
            c.start()
        count = table.shape[1]
        source_bond = first + (site if left else site + 1)
        target_bond = first + (site + 1 if left else site)
        sign = 1 if left else -1
        u = 2 * zpos if left else 2 * zpos + 1
        v = u + sign
        far_u, far_v = u - 2 * sign, v - 2 * sign

        def rows_of(bond, index):
            safe = jnp.clip(index, 0, count - 1)
            return jnp.where((index >= 0) & (index < count), table[bond, safe], 0)

        sub = lax.broadcasted_iota(jnp.int32, (tile, tile), 0)
        lane = lax.broadcasted_iota(jnp.int32, (tile, tile), 1)

        def factor(of_u, state, source, target):
            a = jnp.where(u_near if of_u else jnp.logical_not(u_near), an[state].astype(f32), ac[state].astype(f32))
            a = a if left else a.T
            keep = (sub < rows_of(source_bond, source)) & (lane < rows_of(target_bond, target))
            return jnp.where(keep, a, 0.0)

        for c in factors:
            c.wait()
        if last:
            dual = [factor(False, 3, far_v, v)] + [factor(not left, t, far_v, u) for t in (1, 2)]
            mono = factor(True, 3, far_u, u)
        else:
            dual = [factor(True, 0, u, u)] + [factor(left, t, u, v) for t in (1, 2)]
            mono = factor(False, 0, v, v)
        for i, m in enumerate(dual):
            bd[:, i * tile : (i + 1) * tile] = m.astype(bf16)
        bm[...] = mono.astype(bf16)
        cp[...] = dual[0].T.astype(bf16)
        for i, m in enumerate((dual[1], dual[2], mono)):
            cq[:, i * tile : (i + 1) * tile] = m.T.astype(bf16)

        dual_near = jnp.logical_not(u_near) if last else u_near

        for f in fetches:
            f.wait()
        n = width * GROUP

        def exchange(a, b):
            upper = lax.broadcasted_iota(jnp.int32, a.shape, 1) < GROUP
            return (
                jnp.where(upper, a, pltpu.roll(b, GROUP, 1)),
                jnp.where(upper, pltpu.roll(a, GROUP, 1), b),
            )

        def split(part):
            pairs = part.reshape(width // 2, 2, SUBLANES, tile)
            return jnp.concatenate([h.reshape(n, tile) for h in exchange(pairs[:, 0], pairs[:, 1])], axis=1)

        def joined_rows(part):
            part = part.reshape(width // 2, SUBLANES, 2 * tile)
            a, b = exchange(part[..., :tile], part[..., tile:])
            return jnp.stack([a, b], axis=1).reshape(width, SUBLANES, tile)

        def products(i, slots):
            one, two = slots
            r = pl.ds(pl.multiple_of(i * STEP_ROWS, STEP_ROWS), STEP_ROWS)
            e_n = near[:, r, :]
            e_c = jnp.concatenate([c[:, r, :] for c in crosses], axis=0)
            e_d = jnp.where(dual_near, e_n, e_c).reshape(width * STEP_ROWS, tile)
            e_m = jnp.where(dual_near, e_c, e_n).reshape(width * STEP_ROWS, tile)
            yd = jnp.dot(e_d, bd[...], preferred_element_type=f32).reshape(width, STEP_ROWS, 3 * tile)
            ym = jnp.dot(e_m, bm[...], preferred_element_type=f32).reshape(width, STEP_ROWS, tile)
            for h in range(2):
                c = slice(h * SUBLANES, (h + 1) * SUBLANES)
                one[2 * h] = split(yd[:, c, :tile]).astype(bf16)
                one[2 * h + 1] = split(ym[:, c, :]).astype(bf16)
                two[h] = jnp.concatenate(
                    [split(yd[:, c, t * tile : (t + 1) * tile]) for t in (1, 2)], axis=0
                ).astype(bf16)

        def mix(i, slots):
            one, two = slots
            r = pl.ds(pl.multiple_of(i * STEP_ROWS, STEP_ROWS), STEP_ROWS)

            def put(to, halves):
                z[to, :, r, :] = jnp.concatenate([joined_rows(x) for x in halves], axis=1).astype(bf16)

            for m, to in ((0, 0), (1, 3)):
                put(to, [jnp.dot(ks[...], one[2 * h + m], preferred_element_type=f32)[:n] for h in range(2)])
            mixed = [jnp.dot(kd[...], two[h], preferred_element_type=f32) for h in range(2)]
            for t in range(2):
                put(1 + t, [x[t * n : (t + 1) * n] for x in mixed])

        y0, y1 = (one0, two0), (one1, two1)
        count_rows = tile // STEP_ROWS
        products(0, y0)
        for c in weights:
            c.wait()

        def turn(j, _):
            for k in range(2 // 2):
                i = 2 * j + 2 * k
                products(i + 1, y1)
                mix(i, y0)
                products(jnp.minimum(i + 2, count_rows - 2), y0)
                mix(i + 1, y1)
            return 0

        lax.fori_loop(0, count_rows // 2, turn, 0)
        if last:
            for c in carries:
                c.wait()
        for k in range(3):
            def close(m, _, k=k):
                for i in range(7):
                    at = cuts[k] + 2 * (m * 7 + i)
                    p = jnp.dot(cp[...], jnp.concatenate([z[0, at], z[0, at + 1]], axis=1), preferred_element_type=f32)
                    zq = [z[1:4, at + n].reshape(3 * tile, tile) for n in range(2)]
                    q = jnp.dot(cq[...], jnp.concatenate(zq, axis=1), preferred_element_type=f32)
                    for n in range(2):
                        j = at + n
                        pj, qj = p[:, n * tile : (n + 1) * tile], q[:, n * tile : (n + 1) * tile]
                        if last:
                            pj, qj = pj + vacc[1, j].astype(f32), qj + vacc[0, j].astype(f32)
                            near_j = jnp.where(u_near, qj, pj).astype(bf16)
                            cross_j = jnp.where(u_near, pj, qj).astype(bf16)
                            out_cross[j] = cross_j
                            if out_near is not None:
                                out_near[j] = near_j
                            if out_pair is not None:
                                out_pair[j] = near_j
                                out_pair[width + j] = cross_j
                        else:
                            vacc[0, j] = pj.astype(bf16)
                            vacc[1, j] = qj.astype(bf16)
                return 0

            lax.fori_loop(0, (cuts[k + 1] - cuts[k]) // 14, close, 0)
            if not last:
                carries[2 * k].start()
                carries[2 * k + 1].start()
            elif left:
                saves[k].start()
        for c in saves if last else carries:
            c.wait()


def terms(left, step, steps, info, table, envs, tensors, small, large, acc=None, onto=None):
    tile = envs[0].shape[-1]
    width = small.shape[1] // GROUP
    last = acc is not None
    final = step + 1 == steps
    pieces = len(envs) - 1
    env = pltpu.VMEM((width, tile, tile), bf16)
    total = jax.ShapeDtypeStruct((2, width, tile, tile), bf16)
    n = width * GROUP
    scratch = [
        pltpu.VMEM((tile, 3 * tile), bf16),
        pltpu.VMEM((tile, tile), bf16),
        pltpu.VMEM((tile, tile), bf16),
        pltpu.VMEM((tile, 3 * tile), bf16),
        *[pltpu.VMEM(shape, bf16) for _ in range(2) for shape in ((4, n, 2 * tile), (2, 2 * n, 2 * tile))],
        pltpu.VMEM((4, width, tile, tile), bf16),
        pltpu.VMEM((2, width, tile, tile), bf16),
        pltpu.VMEM((4, tile, tile), bf16),
        pltpu.VMEM((4, tile, tile), bf16),
        pltpu.VMEM(small.shape, bf16),
        pltpu.VMEM(large.shape, bf16),
        pltpu.SemaphoreType.DMA((2, 3)),
        pltpu.SemaphoreType.DMA((4,)),
    ]
    if not last:
        scratch += [pltpu.VMEM((width, tile, tile), bf16)] * 2 + [pltpu.SemaphoreType.DMA((2, 3))]
    operands = [in_vmem(b) if last else b for b in envs] + [*tensors, in_hbm(small), in_hbm(large)]
    info_shape = jax.ShapeDtypeStruct(info.shape, info.dtype)
    out_specs, out_shape = [ANY, SMEM], [total, info_shape]
    aliases = {}
    if last:
        operands.append(acc)
        out_specs, out_shape = [VMEM, SMEM], [env, info_shape]
        if final or not left:
            out_specs.insert(0, VMEM)
            out_shape.insert(0, env)
        if not final:
            out_specs.insert(0, VMEM)
            out_shape.insert(0, pltpu.VMEM((2 * width, tile, tile), bf16))
        if left:
            if onto is not None:
                operands.append(onto)
                aliases = {1 + len(operands): 0}
            out_specs.insert(0, ANY)
            out_shape.insert(0, jax.ShapeDtypeStruct((steps, 1, width, tile, tile), bf16))
            scratch.append(pltpu.SemaphoreType.DMA((3,)))

    def body(info, table, *refs):
        refs = (refs[0], refs[1 : 1 + pieces]) + refs[1 + pieces :]
        terms_body(left, last, final, onto is not None, width, tile, step, steps, info, table, *refs)

    return pl.pallas_call(
        body,
        in_specs=[SMEM, SMEM] + [VMEM if last else ANY] * len(envs) + [ANY] * (len(operands) - len(envs)),
        out_specs=out_specs,
        out_shape=out_shape,
        scratch_shapes=scratch,
        input_output_aliases=aliases,
        compiler_params=pltpu.CompilerParams(vmem_limit_bytes=LIMIT),
    )(info, table, *operands)


def place_body(groups, count, direct, info, *refs):
    pieces = 3
    total = sum(len(sources) for _, _, sources in groups)
    sources, outs, held, sem = refs[:total], refs[-2 - count : -2], refs[-2], refs[-1]
    jobs = []
    for n, (out, index, flags) in enumerate(groups):
        dst = outs[out] if index is None else outs[out].at[index, 0]
        for flag in flags:
            src = sources[len(jobs)]
            cuts = [src.shape[0] * k // pieces for k in range(pieces + 1)]
            spans = [pl.ds(a, b - a) for a, b in zip(cuts, cuts[1:])]
            here = held.at[n]
            reads = [pltpu.make_async_copy(src.at[c], here.at[c], sem.at[0, n, k]) for k, c in enumerate(spans)]
            writes = [pltpu.make_async_copy(here.at[c], dst.at[c], sem.at[1, n, k]) for k, c in enumerate(spans)]
            if direct[len(jobs)]:
                reads, writes = [pltpu.make_async_copy(src.at[c], dst.at[c], sem.at[1, n, k]) for k, c in enumerate(spans)], None
            jobs.append((flag, reads, writes))

    for flag, reads, _ in jobs:

        @pl.when(flag(info))
        def _(reads=reads):
            for c in reads:
                c.start()

    for flag, reads, writes in jobs:

        @pl.when(flag(info))
        def _(reads=reads, writes=writes):
            for a, b in zip(reads, writes or ()):
                a.wait()
                b.start()

    for flag, reads, writes in jobs:

        @pl.when(flag(info))
        def _(reads=reads, writes=writes):
            for c in writes or reads:
                c.wait()


def place(info, groups, shapes, onto, resident=()):
    sources = [b for _, _, pairs in groups for _, b in pairs]
    specs = [VMEM if any(b is r for r in resident) else ANY for b in sources]
    sources = [in_vmem(b) if spec is VMEM else b for b, spec in zip(sources, specs)]
    plan = [(out, index, [flag for flag, _ in pairs]) for out, index, pairs in groups]
    return pl.pallas_call(
        functools.partial(place_body, plan, len(shapes), [spec is VMEM for spec in specs]),
        in_specs=[SMEM] + specs + [ANY] * len(onto),
        out_specs=[ANY] * len(shapes),
        out_shape=[jax.ShapeDtypeStruct(s, bf16) for s in shapes],
        scratch_shapes=[
            pltpu.VMEM((len(groups), *sources[0].shape), bf16),
            pltpu.SemaphoreType.DMA((2, len(groups), 3)),
        ],
        compiler_params=pltpu.CompilerParams(vmem_limit_bytes=LIMIT),
        input_output_aliases={1 + len(sources) + i: i for i in range(len(onto))},
    )(info, *sources, *onto)


def compact(mpo):
    sites, width = mpo.shape[:2]
    return jnp.transpose(mpo, (0, 3, 2, 4, 1)).reshape(sites, 4 * width, 4 * width)


def shards(site_tensors, mpo, left_in, right_in, tile_rows):
    chains, sectors = lax.axis_size("chain"), lax.axis_size("sector")
    routes = Routes(chains, sectors)
    chain, sector = lax.axis_index("chain"), lax.axis_index("sector")
    core, x = chain % 2, sector % 2
    sites, _, tile = site_tensors.shape[:3]
    same = core == x
    info = jnp.stack([(chain - core + x) * sites, sector // 2, x, same.astype(jnp.int32), chain]).astype(jnp.int32)

    left_near, right_own = left_in[0, 0], right_in[0, 0]
    width = left_near.shape[0]
    tensors = jnp.transpose(site_tensors[:, 0], (0, 2, 1, 3)).reshape(sites * 4, tile, tile)
    packed = jnp.concatenate([left_near, tensors])
    left_cross = move(packed, routes.left_cross)
    left_second, right_own, tensors, packed = lax.optimization_barrier((left_near, right_own, tensors, packed))
    left_near_below = move(left_second, routes.left_up)
    right_near_above = move(right_own, routes.right_native_down)
    right_near = move(right_own, routes.to_right_core)
    tensors_below = move(tensors, routes.left_up)
    tensors_right = move(tensors, routes.to_right_core)
    k = compact(mpo)
    k_right = move(k, routes.to_right_core)
    right_own, k_right = lax.optimization_barrier((right_own, k_right))
    cuts = [0, width // 2, width] if width % 2 == 0 else [0, width]
    right_cross = [move(right_own[a:b], routes.right_cross) for a, b in zip(cuts, cuts[1:])]
    ks = spread(info, k, k_right)
    left_cross, left_near_below, right_near_above, ks, tensors_below, tensors_right = lax.optimization_barrier(
        (left_cross, left_near_below, right_near_above, ks, tensors_below, tensors_right)
    )
    left_cross_below = move(left_cross, routes.left_up)
    tensors_cross_right = move(left_cross[width:], routes.to_right_core)
    right_cross_above = [move(b, routes.right_down) for b in right_cross]
    pair, pair_below = (tensors, left_cross), (tensors_below, left_cross_below)
    pair_right = (tensors_right, tensors_cross_right)

    l_far, r_far = (left_near_below, left_cross_below), (right_near_above, *right_cross_above)
    l, r = (in_hbm(left_near), left_cross), (right_near, *right_cross)

    def local(left, step, info, envs, tensors):
        return terms(left, step, sites, info, tile_rows, envs, tensors, ks[3 * step], ks[3 * step + 1])

    def remote(left, step, info, envs, tensors, acc, onto=None):
        return terms(left, step, sites, info, tile_rows, envs, tensors, ks[3 * step + 2], ks[3 * step + 1], acc, onto)

    envs_shape = (sites, 1, width, tile, tile)

    def own(info):
        return info[3] == 1

    def other(info):
        return info[3] != 1

    left_envs = right_envs = None
    kept = []
    info, tensors_cross_right = lax.optimization_barrier((info, tensors_cross_right))
    pair_right = (tensors_right, tensors_cross_right)
    l_acc, info = local(True, 0, info, l, pair)
    for step in range(sites):
        more = step + 1 < sites
        if step > 0:
            kept.append((step, left_back, list(right_back)))
        left_envs, l_first, l_cross, info = remote(True, step, info, l_far, pair_below, l_acc, left_envs)
        left_back = move(l_cross, routes.left_back)
        if more:
            l_far = [move(l_first, routes.left_up)]
        if step == 0:
            r_acc, info = local(False, step, info, r, pair_right)
        if step > 0:
            info, *kept[-1][2][:] = lax.optimization_barrier((info, *kept[-1][2]))
        *r_pair, r_near, r_cross, info = remote(False, step, info, r_far, pair_right, r_acc)
        if more:
            l_acc, info = local(True, step + 1, info, [l_first], pair)
        if more:
            r_far = [move(r_pair[0], routes.right_down)]
            info, left_back = lax.optimization_barrier((info, left_back))
        right_back = (move(r_near, routes.from_right_core), move(r_cross, routes.right_back))
        if more:
            r_acc, info = local(False, step + 1, info, r_pair, pair_right)
    info, left_back = lax.optimization_barrier((info, left_back))
    for step, back, backs in kept:
        left_envs, right_envs = place(
            info,
            [(0, step - 1, [(other, back)]), (1, sites - step, list(zip((own, other), backs)))]
            + ([(0, step, [(other, left_back)])] if step + 1 == sites else []),
            [envs_shape] * 2,
            [left_envs] + ([] if right_envs is None else [right_envs]),
        )

    edge_tile = move(jnp.where(same, l_first, left_back), routes.edge_same + routes.edge_other)
    edge = [
        (lambda info: info[4] == 0, left_in[0, 0]),
        (lambda info: info[4] != 0, edge_tile),
    ]
    left_envs, right_envs, left_edge = place(
        info,
        ([] if kept else [(0, sites - 1, [(other, left_back)])]) + [(1, 0, list(zip((own, other), right_back))), (2, None, edge)],
        [envs_shape, envs_shape, (width, tile, tile)],
        [left_envs] + ([] if right_envs is None else [right_envs]),
        [left_back, *right_back, edge_tile],
    )
    return left_envs, right_envs, left_edge[None, None]


def solution(mesh):
    placed = (
        P("chain", "sector", None, None, None),
        P("chain", None, None, None, None),
        P("chain", "sector", None, None, None),
        P("chain", "sector", None, None, None),
        P(),
    )
    return jax.shard_map(
        shards,
        mesh=mesh,
        in_specs=placed,
        out_specs=(
            P("chain", "sector", None, None, None),
            P("chain", "sector", None, None, None),
            P("chain", "sector", None, None, None),
        ),
        check_vma=False,
    )
```
